32 devices in a mesh: mod: 2 (over y), dp: 16 (over z, x, core).
Axes of the slice: x: 2, y: 2, z: 4, core: 2. Of those that a mesh axis runs over, the one named last changes fastest.
Arguments:
- text_tokens: bfloat16 [24576, 768], P(('mod', 'dp')), may hold values from -6 to 6
- patches: bfloat16 [192, 145, 1024], P(('mod', 'dp')), may hold values from -6 to 6
- lengths: int32 [32, 24], P(('mod', 'dp')), may hold values from 1 to 40, 768 in all within a row
- row_image: int32 [32, 24], P(('mod', 'dp')), may hold values from 0 to 5
- box_mask: int32 [32, 24, 145], P(('mod', 'dp')), may hold values from 0 to 1, as said below
- cotangent: bfloat16 [24576, 768], P(('mod', 'dp')), may hold values from -6 to 6
- self_query: bfloat16 [768, 768], replicated, may hold values from -0.21875 to 0.21875
- self_key: bfloat16 [768, 768], replicated, may hold values from -0.21875 to 0.21875
- self_value: bfloat16 [768, 768], replicated, may hold values from -0.21875 to 0.21875
- self_output: bfloat16 [768, 768], replicated, may hold values from -0.4375 to 0.4375
- first_gain: float32 [768], replicated, may hold values from 0.5 to 1.5
- first_bias: float32 [768], replicated, may hold values from -3 to 3
- cross_query: bfloat16 [768, 768], replicated, may hold values from -0.21875 to 0.21875
- cross_key: bfloat16 [768, 768], replicated, may hold values from -0.21875 to 0.21875
- cross_value: bfloat16 [768, 768], replicated, may hold values from -0.21875 to 0.21875
- cross_output: bfloat16 [768, 768], replicated, may hold values from -0.4375 to 0.4375
- second_gain: float32 [768], replicated, may hold values from 0.5 to 1.5
- second_bias: float32 [768], replicated, may hold values from -3 to 3
- expand_weight: bfloat16 [768, 3072], replicated, may hold values from -0.21875 to 0.21875
- reduce_weight: bfloat16 [3072, 768], replicated, may hold values from -0.109375 to 0.109375
- third_gain: float32 [768], replicated, may hold values from 0.5 to 1.5
- third_bias: float32 [768], replicated, may hold values from -3 to 3
- vision_proj: bfloat16 [1024, 768], replicated, may hold values from -0.1875 to 0.1875
Outputs:
- merged: bfloat16 [24576, 768], P(('mod', 'dp'))
- text_grad: float32 [24576, 768], P(('mod', 'dp'))
- patch_grad: float32 [192, 145, 1024], P(('mod', 'dp'))
- grad_self_query: float32 [768, 768], replicated
- grad_self_key: float32 [768, 768], replicated
- grad_self_value: float32 [768, 768], replicated
- grad_self_output: float32 [768, 768], replicated
- grad_first_gain: float32 [768], replicated
- grad_first_bias: float32 [768], replicated
- grad_cross_query: float32 [768, 768], replicated
- grad_cross_key: float32 [768, 768], replicated
- grad_cross_value: float32 [768, 768], replicated
- grad_cross_output: float32 [768, 768], replicated
- grad_second_gain: float32 [768], replicated
- grad_second_bias: float32 [768], replicated
- grad_expand: float32 [768, 3072], replicated
- grad_reduce: float32 [3072, 768], replicated
- grad_third_gain: float32 [768], replicated
- grad_third_bias: float32 [768], replicated
- grad_vision: float32 [1024, 768], replicated
The draws below stay inside these ranges and needn't reach their ends.
Inputs may be any that keep to these rules, and one draw needn't show every extreme that they name: lengths[b] lists the token counts of the 24 rows packed in order into block b; each row sums to 768. row_image[b, r] is the image, among the 6 images of block (b + 16) mod 32, that row r of block b describes. box_mask[b, r, p] is 1 where row r of block b may attend to patch p of its image; patch 0 is 1 in every row.
All inputs are finite; a program needn't handle non-finite values.
Results may differ from the reference program's by a relative error of at most 0.02.
Values may be sent and summed in bfloat16 or wider, within the bound.
No kernel may reach another device: no remote copies, remote signals or barrier semaphores. Data moves between devices by JAX's collectives and lax.ppermute only.
A program may use at most 384 MiB of HBM per device.

```python
import math
import jax
import jax.numpy as jnp
import numpy as np
from jax import lax

D = 768
HEADS = 12
HEAD_DIM = 64
FF = 3072
DV = 1024
GRID = 12
ML = 40
TOK_DEV = 768
PATCHES = 145
RDEV = 24
IMG_DEV = 6
BLOCKS = 32
TEXT_TOK = 24576
IMAGES = 192
N_DP = 16


def draw_box_mask(key, part):
    key = jax.random.fold_in(key, 11)
    subkeys = jax.random.split(key, 5)
    row_shape = (BLOCKS, RDEV)
    left_edge = jax.random.randint(subkeys[0], row_shape, 0, GRID)
    box_width = jax.random.randint(subkeys[1], row_shape, 1, GRID + 1)
    low_edge = jax.random.randint(subkeys[2], row_shape, 0, GRID)
    box_height = jax.random.randint(subkeys[3], row_shape, 1, GRID + 1)
    is_caption = jax.random.randint(subkeys[4], row_shape, 0, 3) == 0
    grid_place = jnp.arange(GRID * GRID, dtype=jnp.int32)
    column = grid_place % GRID
    grid_line = grid_place // GRID
    inside_x = (column >= left_edge[..., None]) & (column < left_edge[..., None] + box_width[..., None])
    inside_y = (grid_line >= low_edge[..., None]) & (grid_line < low_edge[..., None] + box_height[..., None])
    inside = inside_x & inside_y | is_caption[..., None]
    return jnp.concatenate([jnp.ones(row_shape + (1,), jnp.int32), inside.astype(jnp.int32)], axis=-1)


def touch_ends(drawn, key, smallest, top_value):
    shape = drawn.shape
    spot = [jax.random.randint(jax.random.fold_in(key, axis), (), 0, shape[axis]) for axis in range(len(shape))]
    drawn = drawn.at[tuple(spot)].set(smallest)
    longest = shape.index(max(shape))
    spot[longest] = (spot[longest] + 1) % shape[longest]
    return drawn.at[tuple(spot)].set(top_value)


def block_levels(own_key, dims, pieces, smallest, largest):
    def one(axis_at, shards_of):
        steps = jax.random.uniform(jax.random.fold_in(jax.random.fold_in(own_key, 6), axis_at), (shards_of,), jnp.float32, smallest / len(pieces), largest / len(pieces))
        return jnp.repeat(jnp.exp(steps), dims[axis_at] // shards_of).reshape((-1,) + (1,) * (len(dims) - axis_at - 1))

    gain = one(*pieces[0])
    for cut in pieces[1:]:
        gain = gain * one(*cut)
    return gain


def rank_table(count, lean):
    portions = [(1 << 20) // math.isqrt(standing ** lean) + 1 for standing in range(1, count + 1)]
    deviation = 1 + sum(portions) // (1 << 30)
    return np.cumsum(np.array([max(1, weight // deviation) for weight in portions]))


def skewed_ids(own_key, dims, number_of, slope):
    grid = rank_table(number_of, slope)
    pick = jax.random.randint(jax.random.fold_in(own_key, 1), dims, 0, int(grid[number_of - 1]))
    rank = jnp.searchsorted(jnp.asarray(grid, jnp.int32), pick, side="right")
    return jax.random.permutation(jax.random.fold_in(own_key, 2), number_of)[rank].astype(jnp.int32)


def split_up(amount, total, most, lean):
    portions = [(1 << 20) // math.isqrt(rank ** lean) + 1 for rank in range(2, amount + 1)]
    surplus, counts = total - most - (amount - 1), [1] * (amount - 1)
    while surplus > 0:
        candidates = [i for i in range(amount - 1) if counts[i] < most]
        whole, remaining = sum([portions[i] for i in candidates]), surplus
        for i in candidates:
            more = min(most - counts[i], max(1, remaining * portions[i] // whole), surplus)
            counts[i] = counts[i] + more
            surplus = surplus - more
    return np.array([most] + counts)


def uneven_parts(key, number_of, total, most, slope):
    if number_of == 2:
        one = jax.random.randint(key, (), max(1, total - most), min(most, total - 1) + 1)
        return jnp.stack([one, total - one])
    sizes = jnp.asarray(split_up(number_of, total, most, slope), jnp.int32)
    couples = (number_of - 1) // 2
    giver, taker = sizes[1:1 + 2 * couples:2], sizes[2:2 + 2 * couples:2]
    room = jnp.minimum(giver - 1, most - taker)
    moved = jax.random.randint(jax.random.fold_in(key, 1), (couples,), 0, 1 << 20) % (room + 1)
    sizes = sizes.at[1:1 + 2 * couples:2].set(giver - moved).at[2:2 + 2 * couples:2].set(taker + moved)
    return sizes[jax.random.permutation(jax.random.fold_in(key, 2), number_of)]


def normal_values(key, dims, deviation, reach, pieces=(), kind=jnp.bfloat16):
    array = deviation * jax.random.normal(key, dims, jnp.float32)
    if pieces:
        array = array * block_levels(key, dims, pieces, -0.22, 0.18)
    return jnp.clip(array, -reach, reach).astype(kind)


def setup_inputs(seed: int = 0) -> dict:
    streams_of = jax.random.split(jax.random.key(seed), 24)
    text_tokens = normal_values(streams_of[0], (TEXT_TOK, D), 1.0, 6.0, ((0, 32),))
    patches = normal_values(streams_of[1], (IMAGES, PATCHES, DV), 1.0, 6.0, ((0, 32),))
    lengths = jax.vmap(lambda own: uneven_parts(own, RDEV, TOK_DEV, ML, 2))(jax.random.split(streams_of[2], BLOCKS)).reshape((BLOCKS, RDEV)).astype(jnp.int32)
    row_image = touch_ends(skewed_ids(streams_of[3], (BLOCKS, RDEV), IMG_DEV, 2), jax.random.fold_in(streams_of[3], 3), 0, IMG_DEV - 1).astype(jnp.int32)
    box_mask = draw_box_mask(jax.random.fold_in(streams_of[23], 71), 0)
    cotangent = normal_values(streams_of[5], (TEXT_TOK, D), 1.0, 6.0, ((0, 32),))
    self_query = normal_values(streams_of[6], (D, D), D ** -0.5, 0.21875)
    self_key = normal_values(streams_of[7], (D, D), D ** -0.5, 0.21875)
    self_value = normal_values(streams_of[8], (D, D), D ** -0.5, 0.21875)
    self_output = normal_values(streams_of[9], (D, D), (D // 4) ** -0.5, 0.4375)
    first_gain = jnp.clip(1.0 + 0.1 * jax.random.normal(streams_of[10], (D,), jnp.float32), 0.5, 1.5)
    first_bias = normal_values(streams_of[11], (D,), 0.5, 3.0, (), jnp.float32)
    cross_query = normal_values(streams_of[12], (D, D), D ** -0.5, 0.21875)
    cross_key = normal_values(streams_of[13], (D, D), D ** -0.5, 0.21875)
    cross_value = normal_values(streams_of[14], (D, D), D ** -0.5, 0.21875)
    cross_output = normal_values(streams_of[15], (D, D), (D // 4) ** -0.5, 0.4375)
    second_gain = jnp.clip(1.0 + 0.1 * jax.random.normal(streams_of[16], (D,), jnp.float32), 0.5, 1.5)
    second_bias = normal_values(streams_of[17], (D,), 0.5, 3.0, (), jnp.float32)
    expand_weight = normal_values(streams_of[18], (D, FF), D ** -0.5, 0.21875)
    reduce_weight = normal_values(streams_of[19], (FF, D), FF ** -0.5, 0.109375)
    third_gain = jnp.clip(1.0 + 0.1 * jax.random.normal(streams_of[20], (D,), jnp.float32), 0.5, 1.5)
    third_bias = normal_values(streams_of[21], (D,), 0.5, 3.0, (), jnp.float32)
    vision_proj = normal_values(streams_of[22], (DV, D), DV ** -0.5, 0.1875)
    return {"text_tokens": text_tokens, "patches": patches, "lengths": lengths, "row_image": row_image, "box_mask": box_mask, "cotangent": cotangent, "self_query": self_query, "self_key": self_key, "self_value": self_value, "self_output": self_output, "first_gain": first_gain, "first_bias": first_bias, "cross_query": cross_query, "cross_key": cross_key, "cross_value": cross_value, "cross_output": cross_output, "second_gain": second_gain, "second_bias": second_bias, "expand_weight": expand_weight, "reduce_weight": reduce_weight, "third_gain": third_gain, "third_bias": third_bias, "vision_proj": vision_proj}


@jax.custom_vjp
def low(v):
    return lax.optimization_barrier(v.astype(jnp.bfloat16)).astype(jnp.float32)

@jax.custom_vjp
def low_back(v):
    return v

def low_keep(v):
    return (low(v), None)

def low_pass(kept, grad):
    return (grad,)

def back_keep(v):
    return (v, None)

def back_low(kept, grad):
    return (low(grad),)
low.defvjp(low_keep, low_pass)
low_back.defvjp(back_keep, back_low)
highest = lax.Precision.HIGHEST

def matmul(left, right):
    return jnp.dot(left, right, precision=highest)

def norm_rows(values, gain_row, shift_row):
    centred = values - lax.optimization_barrier(jnp.mean(values, axis=-1, keepdims=True))
    spread = lax.optimization_barrier(jnp.mean(centred * centred, axis=-1, keepdims=True))
    return centred * lax.rsqrt(spread + 1e-05) * gain_row + shift_row

def split_heads(values):
    return values.reshape(values.shape[0], HEADS, HEAD_DIM)

def attend(queries, keys_in, values_in, allowed):
    scores = jnp.einsum('qhd,khd->hqk', split_heads(queries), split_heads(keys_in), precision=highest) * HEAD_DIM ** (-0.5)
    scores = jnp.where(allowed[None], low_back(scores), -1e+30)
    row_top = lax.optimization_barrier(jnp.max(scores, axis=-1, keepdims=True))
    exp_scores = jnp.exp(scores - row_top)
    softmax_out = low(exp_scores / lax.optimization_barrier(jnp.sum(exp_scores, axis=-1, keepdims=True)))
    mixed_heads = jnp.einsum('hqk,khd->qhd', softmax_out, split_heads(values_in), precision=highest)
    return mixed_heads.reshape(queries.shape[0], -1)

def block_masks(row_lengths, row_images, row_boxes):
    row_ends = jnp.cumsum(row_lengths).astype(jnp.int32)
    position = jnp.arange(TOK_DEV, dtype=jnp.int32)
    row_of = lax.optimization_barrier(jnp.sum((position[:, None] >= row_ends[None, :]).astype(jnp.int32), axis=1)).astype(jnp.int32)
    same_row = row_of[:, None] == row_of[None, :]
    choose = (row_of[:, None] == jnp.arange(RDEV, dtype=jnp.int32)[None, :]).astype(jnp.int32)
    token_image = lax.optimization_barrier(jnp.sum(choose * row_images[None, :], axis=1)).astype(jnp.int32)
    token_box = lax.optimization_barrier(jnp.sum(choose[:, :, None] * row_boxes[None, :, :], axis=1)).astype(jnp.int32)
    key_image = jnp.arange(IMG_DEV * PATCHES, dtype=jnp.int32) // PATCHES
    cross_allowed = (token_image[:, None] == key_image[None, :]) & (jnp.tile(token_box, (1, IMG_DEV)) > 0)
    return (same_row, cross_allowed)

def encoder_layer(text_all, patch_all, weight_all, lengths, row_image, box_mask):
    self_query, self_key, self_value, self_output, first_gain, first_bias, cross_query, cross_key, cross_value, cross_output, second_gain, second_bias, expand_weight, reduce_weight, third_gain, third_bias, vision_proj = weight_all
    text_blocks = text_all.reshape(BLOCKS, TOK_DEV, D)
    partner_patches = jnp.roll(patch_all.reshape(BLOCKS, IMG_DEV * PATCHES, DV), -N_DP, axis=0)

    def one_block(inputs):
        tokens, patch_rows, row_lengths, row_images, row_boxes = inputs
        same_row, cross_allowed = block_masks(row_lengths, row_images, row_boxes)
        projected = low_back(low(matmul(patch_rows, vision_proj)))
        cross_keys = low_back(low(matmul(projected, cross_key)))
        cross_values = low_back(low(matmul(projected, cross_value)))
        query_s = low_back(low(matmul(tokens, self_query)))
        key_s = low_back(low(matmul(tokens, self_key)))
        value_s = low_back(low(matmul(tokens, self_value)))
        attended = low_back(low(attend(query_s, key_s, value_s, same_row)))
        first_sum = tokens + low_back(matmul(attended, self_output))
        normed_one = norm_rows(first_sum, first_gain, first_bias)
        query_c = low_back(low(matmul(low(normed_one), cross_query)))
        crossed = low_back(low(attend(query_c, cross_keys, cross_values, cross_allowed)))
        second_sum = normed_one + low_back(matmul(crossed, cross_output))
        normed_two = norm_rows(second_sum, second_gain, second_bias)
        hidden = low_back(matmul(low(normed_two), expand_weight))
        activated = low(jax.nn.gelu(hidden, approximate=False))
        third_sum = normed_two + low_back(matmul(activated, reduce_weight))
        return norm_rows(third_sum, third_gain, third_bias)
    outputs = lax.map(jax.checkpoint(one_block), (text_blocks, partner_patches, lengths, row_image, box_mask))
    return outputs.reshape(TEXT_TOK, D)

def reference(text_tokens, patches, lengths, row_image, box_mask, cotangent, self_query, self_key, self_value, self_output, first_gain, first_bias, cross_query, cross_key, cross_value, cross_output, second_gain, second_bias, expand_weight, reduce_weight, third_gain, third_bias, vision_proj):
    weight_all = tuple((w.astype(jnp.float32) for w in (self_query, self_key, self_value, self_output, first_gain, first_bias, cross_query, cross_key, cross_value, cross_output, second_gain, second_bias, expand_weight, reduce_weight, third_gain, third_bias, vision_proj)))

    def forward(text_all, patch_all, weight_set):
        return encoder_layer(text_all, patch_all, weight_set, lengths, row_image, box_mask)
    merged, pullback = jax.vjp(forward, text_tokens.astype(jnp.float32), patches.astype(jnp.float32), weight_all)
    text_grad, patch_grad, weight_grads = pullback(cotangent.astype(jnp.float32))
    return (merged.astype(jnp.bfloat16), text_grad, patch_grad, weight_grads[0], weight_grads[1], weight_grads[2], weight_grads[3], weight_grads[4], weight_grads[5], weight_grads[6], weight_grads[7], weight_grads[8], weight_grads[9], weight_grads[10], weight_grads[11], weight_grads[12], weight_grads[13], weight_grads[14], weight_grads[15], weight_grads[16])
```

```python
import jax
import jax.numpy as jnp
from jax import lax
from jax.sharding import PartitionSpec as P

HEADS = 12
HEAD_DIM = 64
TOK_DEV = 768


def from_partner(block, axis, bit):
    count = lax.axis_size(axis)
    route = []
    for low in range(count):
        high = low | 1 << bit
        if high != low and high < count:
            route += [(low, high), (high, low)]
    return lax.ppermute(block, axis, route)


def norm_rows(values, gain_row, shift_row):
    centred = values - jnp.mean(values, axis=-1, keepdims=True)
    spread = jnp.mean(centred * centred, axis=-1, keepdims=True)
    return centred * lax.rsqrt(spread + 1e-05) * gain_row + shift_row


def gelu_exact(values):
    return jax.nn.gelu(values, approximate=False)


def matmul(left, right):
    return jnp.dot(left, right, preferred_element_type=jnp.float32)


def matmul_left_t(left, right):
    return lax.dot_general(
        left, right, (((0,), (0,)), ((), ())), preferred_element_type=jnp.float32
    )


def matmul_right_t(left, right):
    return lax.dot_general(
        left, right, (((1,), (1,)), ((), ())), preferred_element_type=jnp.float32
    )


def split_heads(values):
    return values.reshape(values.shape[0], HEADS, HEAD_DIM)


def head_scores(queries, keys_in, allowed):
    raw_scores = jnp.einsum(
        "qhd,khd->hqk",
        split_heads(queries),
        split_heads(keys_in),
        preferred_element_type=jnp.float32,
    ) * HEAD_DIM ** (-0.5)
    return jnp.where(allowed[None], raw_scores, -1e30)


def attend_forward(queries, keys_in, values_in, allowed):
    scores = head_scores(queries, keys_in, allowed)
    row_top = jnp.max(scores, axis=-1, keepdims=True)
    exp_scores = jnp.exp(scores - row_top)
    row_total = jnp.sum(exp_scores, axis=-1, keepdims=True)
    softmax_out = (exp_scores / row_total).astype(jnp.bfloat16)
    mixed_heads = jnp.einsum(
        "hqk,khd->qhd", softmax_out, split_heads(values_in), preferred_element_type=jnp.float32
    )
    return (mixed_heads.reshape(queries.shape[0], -1), row_top + jnp.log(row_total))


def attend_backward(queries, keys_in, values_in, allowed, log_total, grad_mixed):
    scores = head_scores(queries, keys_in, allowed)
    softmax_out = jnp.exp(scores - log_total)
    grad_heads = split_heads(grad_mixed)
    grad_soft = jnp.einsum(
        "qhd,khd->hqk", grad_heads, split_heads(values_in), preferred_element_type=jnp.float32
    )
    row_inner = jnp.sum(softmax_out * grad_soft, axis=-1, keepdims=True)
    grad_scores = (softmax_out * (grad_soft - row_inner)).astype(jnp.bfloat16)
    grad_queries = jnp.einsum(
        "hqk,khd->qhd", grad_scores, split_heads(keys_in), preferred_element_type=jnp.float32
    ) * HEAD_DIM ** (-0.5)
    grad_keys = jnp.einsum(
        "hqk,qhd->khd", grad_scores, split_heads(queries), preferred_element_type=jnp.float32
    ) * HEAD_DIM ** (-0.5)
    grad_values = jnp.einsum(
        "hqk,qhd->khd",
        softmax_out.astype(jnp.bfloat16),
        grad_heads,
        preferred_element_type=jnp.float32,
    )
    return (
        grad_queries.reshape(queries.shape[0], -1).astype(jnp.bfloat16),
        grad_keys.reshape(keys_in.shape[0], -1).astype(jnp.bfloat16),
        grad_values.reshape(keys_in.shape[0], -1).astype(jnp.bfloat16),
    )


def block_masks(row_lengths, row_images, row_boxes, image_count):
    row_ends = jnp.cumsum(row_lengths)
    position = jnp.arange(TOK_DEV, dtype=jnp.int32)
    row_of = jnp.sum((position[:, None] >= row_ends[None, :]).astype(jnp.int32), axis=1)
    same_row = row_of[:, None] == row_of[None, :]
    choose = (row_of[:, None] == jnp.arange(row_lengths.shape[0], dtype=jnp.int32)[None, :]).astype(
        jnp.int32
    )
    token_image = jnp.sum(choose * row_images[None, :], axis=1)
    token_box = jnp.sum(choose[:, :, None] * row_boxes[None, :, :], axis=1)
    patch_count = row_boxes.shape[1]
    key_image = jnp.arange(image_count * patch_count, dtype=jnp.int32) // patch_count
    cross_allowed = (token_image[:, None] == key_image[None, :]) & (
        jnp.tile(token_box, (1, image_count)) > 0
    )
    return (same_row, cross_allowed)


def flip_bit(values, axis, bit):
    count = lax.axis_size(axis)
    return lax.ppermute(values, axis, [(i, i ^ (1 << bit)) for i in range(count)])


def my_bit(axis, bit):
    return (lax.axis_index(axis) >> bit) & 1


def stage_orders():
    dp_bits = lax.axis_size("dp").bit_length() - 1
    mod_bits = lax.axis_size("mod").bit_length() - 1
    core = [("dp", 0)]
    near = [("dp", 1)]
    across = [("mod", bit) for bit in range(mod_bits)]
    rest = [("dp", bit) for bit in range(2, dp_bits)]
    return (core + near + across + rest, core + across + near + rest)


def halves(values, dim):
    shape = values.shape
    return values.reshape(shape[:dim] + (2, shape[dim] // 2) + shape[dim + 1 :])


def sum_scatter(values, order):
    for step, (axis, bit) in enumerate(order):
        if step >= 5:
            values = values + flip_bit(values, axis, bit)
            continue
        dim = 0 if values.shape[0] % 32 == 0 else 1
        pair = halves(values, dim)
        mine = my_bit(axis, bit)
        away = lax.dynamic_index_in_dim(pair, 1 - mine, dim, False)
        keep = lax.dynamic_index_in_dim(pair, mine, dim, False)
        values = keep + flip_bit(away, axis, bit)
    return values


def gather_back(values, order, shape):
    dims = []
    rows, columns = shape
    for step in range(min(5, len(order))):
        dim = 0 if rows % 32 == 0 else 1
        rows, columns = (rows // 2, columns) if dim == 0 else (rows, columns // 2)
        dims.append(dim)
    for step in reversed(range(len(dims))):
        axis, bit = order[step]
        other = flip_bit(values, axis, bit)
        low = my_bit(axis, bit) == 0
        if step == 0:
            values, other = values.astype(jnp.float32), other.astype(jnp.float32)
        values = jnp.concatenate(
            [jnp.where(low, values, other), jnp.where(low, other, values)], axis=dims[step]
        )
    return values


def total(values, order):
    values = values.astype(jnp.bfloat16)
    return gather_back(sum_scatter(values, order), order, values.shape)


def on_device(
    text_tokens,
    patches,
    lengths,
    row_image,
    box_mask,
    cotangent,
    self_query,
    self_key,
    self_value,
    self_output,
    first_gain,
    first_bias,
    cross_query,
    cross_key,
    cross_value,
    cross_output,
    second_gain,
    second_bias,
    expand_weight,
    reduce_weight,
    third_gain,
    third_bias,
    vision_proj,
):
    image_count = patches.shape[0]
    same_row, cross_allowed = block_masks(lengths[0], row_image[0], box_mask[0], image_count)
    flat_patches = patches.reshape(image_count * patches.shape[1], patches.shape[2])
    projected = matmul(flat_patches, vision_proj).astype(jnp.bfloat16)
    own_keys = matmul(projected, cross_key).astype(jnp.bfloat16)
    own_values = matmul(projected, cross_value).astype(jnp.bfloat16)
    far_keys, far_values = from_partner((own_keys, own_values), "mod", 0)
    query_s = matmul(text_tokens, self_query).astype(jnp.bfloat16)
    key_s = matmul(text_tokens, self_key).astype(jnp.bfloat16)
    value_s = matmul(text_tokens, self_value).astype(jnp.bfloat16)
    attended, self_log = attend_forward(query_s, key_s, value_s, same_row)
    attended_b = attended.astype(jnp.bfloat16)
    first_sum = text_tokens.astype(jnp.float32) + matmul(attended_b, self_output)
    normed_one, first_back = jax.vjp(norm_rows, first_sum, first_gain, first_bias)
    normed_one_b = normed_one.astype(jnp.bfloat16)
    query_c = matmul(normed_one_b, cross_query).astype(jnp.bfloat16)
    crossed, cross_log = attend_forward(query_c, far_keys, far_values, cross_allowed)
    crossed_b = crossed.astype(jnp.bfloat16)
    second_sum = normed_one + matmul(crossed_b, cross_output)
    normed_two, second_back = jax.vjp(norm_rows, second_sum, second_gain, second_bias)
    normed_two_b = normed_two.astype(jnp.bfloat16)
    hidden = matmul(normed_two_b, expand_weight)
    activated, gelu_back = jax.vjp(gelu_exact, hidden)
    activated_b = activated.astype(jnp.bfloat16)
    third_sum = normed_two + matmul(activated_b, reduce_weight)
    normed_three, third_back = jax.vjp(norm_rows, third_sum, third_gain, third_bias)
    merged = normed_three.astype(jnp.bfloat16)
    grad_third, grad_third_gain, grad_third_bias = third_back(cotangent.astype(jnp.float32))
    grad_third_b = grad_third.astype(jnp.bfloat16)
    grad_reduce = matmul_left_t(activated_b, grad_third_b)
    grad_active = matmul_right_t(grad_third_b, reduce_weight)
    grad_hidden = gelu_back(grad_active)[0].astype(jnp.bfloat16)
    grad_expand = matmul_left_t(normed_two_b, grad_hidden)
    grad_normed_two = grad_third + matmul_right_t(grad_hidden, expand_weight)
    grad_second, grad_second_gain, grad_second_bias = second_back(grad_normed_two)
    grad_second_b = grad_second.astype(jnp.bfloat16)
    grad_cross_output = matmul_left_t(crossed_b, grad_second_b)
    grad_crossed = matmul_right_t(grad_second_b, cross_output).astype(jnp.bfloat16)
    grad_query_c, grad_far_keys, grad_far_values = attend_backward(
        query_c, far_keys, far_values, cross_allowed, cross_log, grad_crossed
    )
    grad_cross_query = matmul_left_t(normed_one_b, grad_query_c)
    grad_normed_one = grad_second + matmul_right_t(grad_query_c, cross_query)
    grad_first, grad_first_gain, grad_first_bias = first_back(grad_normed_one)
    grad_first_b = grad_first.astype(jnp.bfloat16)
    grad_self_output = matmul_left_t(attended_b, grad_first_b)
    grad_attended = matmul_right_t(grad_first_b, self_output).astype(jnp.bfloat16)
    grad_query_s, grad_key_s, grad_value_s = attend_backward(
        query_s, key_s, value_s, same_row, self_log, grad_attended
    )
    grad_self_query = matmul_left_t(text_tokens, grad_query_s)
    grad_self_key = matmul_left_t(text_tokens, grad_key_s)
    grad_self_value = matmul_left_t(text_tokens, grad_value_s)
    text_grad = (
        grad_first
        + matmul_right_t(grad_query_s, self_query)
        + matmul_right_t(grad_key_s, self_key)
        + matmul_right_t(grad_value_s, self_value)
    )
    back_keys, back_values = from_partner((grad_far_keys, grad_far_values), "mod", 0)
    grad_cross_key = matmul_left_t(projected, back_keys)
    grad_cross_value = matmul_left_t(projected, back_values)
    grad_projected = (
        matmul_right_t(back_keys, cross_key) + matmul_right_t(back_values, cross_value)
    ).astype(jnp.bfloat16)
    grad_vision = matmul_left_t(flat_patches, grad_projected)
    patch_grad = matmul_right_t(grad_projected, vision_proj).reshape(patches.shape)
    one_way, other_way = stage_orders()
    half_ff = grad_reduce.shape[0] // 2
    sum_reduce = jnp.concatenate(
        [total(grad_reduce[:half_ff], one_way), total(grad_reduce[half_ff:], other_way)], axis=0
    )
    sum_expand = jnp.concatenate(
        [total(grad_expand[:, :half_ff], one_way), total(grad_expand[:, half_ff:], other_way)],
        axis=1,
    )
    width = grad_cross_query.shape[1]

    def couple(left, right, order):
        both = total(jnp.concatenate([left, right], axis=1), order)
        return both[:, :width], both[:, width:]

    sum_cross_output, sum_cross_query = couple(grad_cross_output, grad_cross_query, one_way)
    sum_cross_key, sum_cross_value = couple(grad_cross_key, grad_cross_value, other_way)
    sum_vision = total(grad_vision, one_way)
    sum_self_output, sum_self_query = couple(grad_self_output, grad_self_query, other_way)
    sum_self_key, sum_self_value = couple(grad_self_key, grad_self_value, one_way)
    small = lax.psum(
        jnp.stack(
            [
                grad_first_gain,
                grad_first_bias,
                grad_second_gain,
                grad_second_bias,
                grad_third_gain,
                grad_third_bias,
            ]
        ),
        ("mod", "dp"),
    )
    return (
        merged,
        text_grad,
        patch_grad,
        sum_self_query,
        sum_self_key,
        sum_self_value,
        sum_self_output,
        small[0],
        small[1],
        sum_cross_query,
        sum_cross_key,
        sum_cross_value,
        sum_cross_output,
        small[2],
        small[3],
        sum_expand,
        sum_reduce,
        small[4],
        small[5],
        sum_vision,
    )


def solution(mesh):
    placed = (
        P(("mod", "dp"), None),
        P(("mod", "dp"), None, None),
        P(("mod", "dp"), None),
        P(("mod", "dp"), None),
        P(("mod", "dp"), None, None),
        P(("mod", "dp"), None),
        P(),
        P(),
        P(),
        P(),
        P(),
        P(),
        P(),
        P(),
        P(),
        P(),
        P(),
        P(),
        P(),
        P(),
        P(),
        P(),
        P(),
    )
    return jax.shard_map(
        on_device,
        mesh=mesh,
        in_specs=placed,
        out_specs=(
            P(("mod", "dp"), None),
            P(("mod", "dp"), None),
            P(("mod", "dp"), None, None),
            P(),
            P(),
            P(),
            P(),
            P(),
            P(),
            P(),
            P(),
            P(),
            P(),
            P(),
            P(),
            P(),
            P(),
            P(),
            P(),
            P(),
        ),
        check_vma=False,
    )
```

```python
import functools

import jax
import jax.numpy as jnp
from jax import lax
from jax.experimental import pallas as pl
from jax.experimental.pallas import tpu as pltpu
from jax.sharding import PartitionSpec as P

HEAD_DIM = 64
TOK_DEV = 768
PATCH_ROWS = 160
LONGEST = 40
WINDOW = 64
SLOTS = 128
LANES = 256
BASES = (0, 128, 384, 512)
TOGETHER = 4


def from_partner(block, axis, bit):
    count = lax.axis_size(axis)
    route = []
    for low in range(count):
        high = low | 1 << bit
        if high != low and high < count:
            route += [(low, high), (high, low)]
    return lax.ppermute(block, axis, route)


def norm_rows(values, gain_row, shift_row):
    centred = values - jnp.mean(values, axis=-1, keepdims=True)
    spread = jnp.mean(centred * centred, axis=-1, keepdims=True)
    return centred * lax.rsqrt(spread + 1e-05) * gain_row + shift_row


def gelu_exact(values):
    return jax.nn.gelu(values, approximate=False)


def matmul(left, right):
    return jnp.dot(left, right, preferred_element_type=jnp.float32)


def matmul_left_t(left, right):
    return lax.dot_general(
        left, right, (((0,), (0,)), ((), ())), preferred_element_type=jnp.float32
    )


def matmul_right_t(left, right):
    return lax.dot_general(
        left, right, (((1,), (1,)), ((), ())), preferred_element_type=jnp.float32
    )


def slot_of(shape, dim):
    slot = lax.broadcasted_iota(jnp.int32, shape, dim)
    part = (slot >= LONGEST).astype(jnp.int32) + (slot >= 2 * LONGEST).astype(jnp.int32)
    return part, slot - part * LONGEST


def fill_head_masks(masks_ref):
    part, _ = slot_of((SLOTS, LANES), 0)
    lane = lax.broadcasted_iota(jnp.int32, (SLOTS, LANES), 1)
    for odd in range(2):
        low = HEAD_DIM * (part + odd)
        inside = (lane >= low) & (lane < low + HEAD_DIM)
        masks_ref[odd] = jnp.where(inside, 1.0, 0.0).astype(jnp.bfloat16)


def row_place(start):
    first = jnp.minimum(lax.bitwise_and(start, -16), TOK_DEV - WINDOW)
    return pl.multiple_of(first, 16), start - first


def pick_rows(offset, length):
    _, place = slot_of((SLOTS, WINDOW), 0)
    at = lax.broadcasted_iota(jnp.int32, (SLOTS, WINDOW), 1)
    return jnp.where((place < length) & (at == place + offset), 1.0, 0.0).astype(jnp.bfloat16)


def put_rows(offset, length):
    _, place = slot_of((WINDOW, SLOTS), 1)
    at = lax.broadcasted_iota(jnp.int32, (WINDOW, SLOTS), 0)
    return jnp.where((place < length) & (at == place + offset), 1.0, 0.0).astype(jnp.bfloat16)


def dot(left, right, over):
    return lax.dot_general(left, right, (over, ((), ())), preferred_element_type=jnp.float32)


NT = ((1,), (1,))
NN = ((1,), (0,))
TN = ((0,), (0,))


def side_by_side(parts):
    first, second, third, fourth = parts
    half = LANES // 2
    return jnp.concatenate(
        [
            first[:, :half],
            first[:, half:] + second[:, :half],
            second[:, half:],
            third[:, :half],
            third[:, half:] + fourth[:, :half],
            fourth[:, half:],
        ],
        axis=1,
    )


def self_allowed(offset, length):
    at = lax.broadcasted_iota(jnp.int32, (WINDOW, SLOTS), 0)
    return (at >= offset) & (at < offset + length)


def cross_allowed(box_ref, row):
    turn = lax.broadcasted_iota(jnp.int32, (SLOTS, SLOTS), 0)
    chosen = jnp.where(turn == row, 1.0, 0.0).astype(jnp.bfloat16)
    return dot(box_ref[...], chosen, NN) > 0.5


def row_keys(cross, first, image, ref, base):
    if cross:
        return ref[image, :, base : base + LANES]
    return ref[pl.ds(first, WINDOW), base : base + LANES]


def forward_kernel(cross, *refs):
    if cross:
        lengths, images, box_ref, q_ref, k_ref, v_ref, out_ref, log_ref, masks, total = refs
    else:
        lengths, q_ref, k_ref, v_ref, out_ref, log_ref, masks, total = refs
        images = box_ref = None
    fill_head_masks(masks)
    total[...] = jnp.zeros_like(total)

    def rows_at_once(step, start):
        work = []
        for turn in range(TOGETHER):
            row = TOGETHER * step + turn
            length = lengths[0, row]
            first, offset = row_place(start)
            work.append((row, length, images[0, row] if cross else None, first, offset))
            start = start + length
        picked = [
            dot(pick_rows(offset, length), q_ref[pl.ds(first, WINDOW), :], NN)
            for _, length, _, first, offset in work
        ]
        picked = [(p * HEAD_DIM ** (-0.5)).astype(jnp.bfloat16) for p in picked]
        allowed = [
            cross_allowed(box_ref, row) if cross else self_allowed(offset, length)
            for row, length, _, _, offset in work
        ]
        each = [(turn, group) for turn in range(TOGETHER) for group in range(len(BASES))]
        scores = {}
        for turn, group in each:
            _, _, image, first, _ = work[turn]
            base = BASES[group]
            queries = picked[turn][:, base : base + LANES] * masks[group % 2]
            keys_in = row_keys(cross, first, image, k_ref, base)
            scores[turn, group] = dot(keys_in, queries, NT)
        soft = {}
        for turn, group in each:
            row = work[turn][0]
            masked = jnp.where(allowed[turn], scores[turn, group], -1e30)
            top = jnp.max(masked, axis=0, keepdims=True)
            exps = jnp.exp(masked - top)
            summed = jnp.sum(exps, axis=0, keepdims=True)
            soft[turn, group] = (exps * (1.0 / summed)).astype(jnp.bfloat16)
            log_ref[row, group : group + 1, :] = top + jnp.log(summed)
        mixed = {}
        for turn, group in each:
            _, _, image, first, _ = work[turn]
            values_in = row_keys(cross, first, image, v_ref, BASES[group])
            mixed[turn, group] = (
                dot(soft[turn, group], values_in, TN).astype(jnp.bfloat16) * masks[group % 2]
            )
        for turn in range(TOGETHER):
            _, length, _, first, offset = work[turn]
            side = side_by_side([mixed[turn, group] for group in range(len(BASES))])
            total[pl.ds(first, WINDOW), :] += dot(put_rows(offset, length), side, NN)
        return start

    rows = lengths.shape[1]
    lax.fori_loop(0, rows // TOGETHER, rows_at_once, jnp.int32(0))
    out_ref[...] = total[...].astype(out_ref.dtype)


def backward_kernel(cross, *refs):
    if cross:
        lengths, images, box_ref = refs[:3]
        refs = refs[3:]
    else:
        lengths, refs = refs[0], refs[1:]
        images = box_ref = None
    q_ref, k_ref, v_ref, g_ref, log_ref, dq_ref, dk_ref, dv_ref, masks, dq, dk, dv = refs
    fill_head_masks(masks)
    dq[...] = jnp.zeros_like(dq)
    dk[...] = jnp.zeros_like(dk)
    dv[...] = jnp.zeros_like(dv)

    def rows_at_once(step, start):
        work = []
        for turn in range(TOGETHER):
            row = TOGETHER * step + turn
            length = lengths[0, row]
            first, offset = row_place(start)
            work.append((row, length, images[0, row] if cross else None, first, offset))
            start = start + length
        picks = [pick_rows(offset, length) for _, length, _, _, offset in work]
        picked = [
            (dot(pick, q_ref[pl.ds(w[3], WINDOW), :], NN) * HEAD_DIM ** (-0.5)).astype(jnp.bfloat16)
            for pick, w in zip(picks, work)
        ]
        picked_g = [
            dot(pick, g_ref[pl.ds(w[3], WINDOW), :], NN).astype(jnp.bfloat16)
            for pick, w in zip(picks, work)
        ]
        allowed = [
            cross_allowed(box_ref, row) if cross else self_allowed(offset, length)
            for row, length, _, _, offset in work
        ]
        each = [(turn, group) for turn in range(TOGETHER) for group in range(len(BASES))]
        queries, grads, scores, grad_soft = {}, {}, {}, {}
        for turn, group in each:
            _, _, image, first, _ = work[turn]
            base = BASES[group]
            mask = masks[group % 2]
            queries[turn, group] = picked[turn][:, base : base + LANES] * mask
            grads[turn, group] = picked_g[turn][:, base : base + LANES] * mask
            keys_in = row_keys(cross, first, image, k_ref, base)
            values_in = row_keys(cross, first, image, v_ref, base)
            scores[turn, group] = dot(keys_in, queries[turn, group], NT)
            grad_soft[turn, group] = dot(values_in, grads[turn, group], NT)
        soft, grad_scores = {}, {}
        for turn, group in each:
            row = work[turn][0]
            masked = jnp.where(allowed[turn], scores[turn, group], -1e30)
            kept = jnp.exp(masked - log_ref[row, group : group + 1, :])
            inner = jnp.sum(kept * grad_soft[turn, group], axis=0, keepdims=True)
            grad_scores[turn, group] = (kept * (grad_soft[turn, group] - inner)).astype(
                jnp.bfloat16
            )
            soft[turn, group] = kept.astype(jnp.bfloat16)
        grad_k, grad_v, grad_q = {}, {}, {}
        for turn, group in each:
            _, _, image, first, _ = work[turn]
            keys_in = row_keys(cross, first, image, k_ref, BASES[group])
            grad_k[turn, group] = dot(grad_scores[turn, group], queries[turn, group], NN)
            grad_v[turn, group] = dot(soft[turn, group], grads[turn, group], NN)
            grad_q[turn, group] = (
                dot(grad_scores[turn, group], keys_in, TN) * HEAD_DIM ** (-0.5)
            ).astype(jnp.bfloat16) * masks[group % 2]
        for turn in range(TOGETHER):
            _, length, image, first, offset = work[turn]
            every = range(len(BASES))
            side_k = side_by_side([grad_k[turn, group] for group in every])
            side_v = side_by_side([grad_v[turn, group] for group in every])
            side_q = side_by_side([grad_q[turn, group] for group in every])
            if cross:
                dk[image] += side_k
                dv[image] += side_v
            else:
                dk[pl.ds(first, WINDOW), :] += side_k
                dv[pl.ds(first, WINDOW), :] += side_v
            dq[pl.ds(first, WINDOW), :] += dot(put_rows(offset, length), side_q, NN)
        return start

    rows = lengths.shape[1]
    lax.fori_loop(0, rows // TOGETHER, rows_at_once, jnp.int32(0))
    dq_ref[...] = dq[...].astype(dq_ref.dtype)
    dk_ref[...] = dk[...].astype(dk_ref.dtype)
    dv_ref[...] = dv[...].astype(dv_ref.dtype)


def in_smem():
    return pl.BlockSpec(memory_space=pltpu.SMEM)


def in_vmem():
    return pl.BlockSpec(memory_space=pltpu.VMEM)


def attend(scalars, queries, keys_in, values_in, box):
    cross = box is not None
    rows = scalars[0].shape[1]
    tensors = ((box,) if cross else ()) + (queries, keys_in, values_in)
    return pl.pallas_call(
        functools.partial(forward_kernel, cross),
        out_shape=(
            jax.ShapeDtypeStruct(queries.shape, jnp.bfloat16),
            jax.ShapeDtypeStruct((rows, len(BASES), SLOTS), jnp.float32),
        ),
        in_specs=[in_smem()] * len(scalars) + [in_vmem()] * len(tensors),
        out_specs=(in_vmem(), in_vmem()),
        scratch_shapes=[
            pltpu.VMEM((2, SLOTS, LANES), jnp.bfloat16),
            pltpu.VMEM(queries.shape, jnp.float32),
        ],
        compiler_params=pltpu.CompilerParams(vmem_limit_bytes=40 << 20),
        cost_estimate=pl.CostEstimate(flops=8 << 30, bytes_accessed=6 << 20, transcendentals=1 << 21),
        name="cross_attend" if cross else "self_attend",
    )(*scalars, *tensors)


def attend_back(scalars, queries, keys_in, values_in, grads, logs, box):
    cross = box is not None
    tensors = ((box,) if cross else ()) + (queries, keys_in, values_in, grads, logs)
    return pl.pallas_call(
        functools.partial(backward_kernel, cross),
        out_shape=tuple(
            jax.ShapeDtypeStruct(a.shape, jnp.bfloat16) for a in (queries, keys_in, values_in)
        ),
        in_specs=[in_smem()] * len(scalars) + [in_vmem()] * len(tensors),
        out_specs=(in_vmem(),) * 3,
        scratch_shapes=[
            pltpu.VMEM((2, SLOTS, LANES), jnp.bfloat16),
            pltpu.VMEM(queries.shape, jnp.float32),
            pltpu.VMEM(keys_in.shape, jnp.float32),
            pltpu.VMEM(keys_in.shape, jnp.float32),
        ],
        compiler_params=pltpu.CompilerParams(vmem_limit_bytes=48 << 20),
        cost_estimate=pl.CostEstimate(flops=20 << 30, bytes_accessed=12 << 20, transcendentals=1 << 21),
        name="cross_attend_back" if cross else "self_attend_back",
    )(*scalars, *tensors)


def box_columns(box_mask, patch_rows):
    turned = jnp.transpose(box_mask).astype(jnp.bfloat16)
    return jnp.pad(
        turned, ((0, patch_rows - turned.shape[0]), (0, SLOTS - turned.shape[1]))
    )


def flip_bit(values, axis, bit):
    count = lax.axis_size(axis)
    return lax.ppermute(values, axis, [(i, i ^ (1 << bit)) for i in range(count)])


def my_bit(axis, bit):
    return (lax.axis_index(axis) >> bit) & 1


def stage_orders():
    dp_bits = lax.axis_size("dp").bit_length() - 1
    mod_bits = lax.axis_size("mod").bit_length() - 1
    core = [("dp", 0)]
    near = [("dp", 1)]
    across = [("mod", bit) for bit in range(mod_bits)]
    rest = [("dp", bit) for bit in range(2, dp_bits)]
    return (core + near + across + rest, core + across + near + rest)


def halves(values, dim):
    shape = values.shape
    return values.reshape(shape[:dim] + (2, shape[dim] // 2) + shape[dim + 1 :])


def sum_scatter(values, order):
    for step, (axis, bit) in enumerate(order):
        if step >= 5:
            values = values + flip_bit(values, axis, bit)
            continue
        dim = 0 if values.shape[0] % 32 == 0 else 1
        pair = halves(values, dim)
        mine = my_bit(axis, bit)
        away = lax.dynamic_index_in_dim(pair, 1 - mine, dim, False)
        keep = lax.dynamic_index_in_dim(pair, mine, dim, False)
        values = keep + flip_bit(away, axis, bit)
    return values


def gather_back(values, order, shape):
    dims = []
    rows, columns = shape
    for step in range(min(5, len(order))):
        dim = 0 if rows % 32 == 0 else 1
        rows, columns = (rows // 2, columns) if dim == 0 else (rows, columns // 2)
        dims.append(dim)
    for step in reversed(range(len(dims))):
        axis, bit = order[step]
        other = flip_bit(values, axis, bit)
        low = my_bit(axis, bit) == 0
        if step == 0:
            values, other = values.astype(jnp.float32), other.astype(jnp.float32)
        values = jnp.concatenate(
            [jnp.where(low, values, other), jnp.where(low, other, values)], axis=dims[step]
        )
    return values


def sum_everywhere(values):
    order, _ = stage_orders()
    for axis, bit in order:
        values = values + flip_bit(values, axis, bit)
    return values


def total(values, order):
    values = values.astype(jnp.bfloat16)
    return gather_back(sum_scatter(values, order), order, values.shape)


def on_device(
    text_tokens,
    patches,
    lengths,
    row_image,
    box_mask,
    cotangent,
    self_query,
    self_key,
    self_value,
    self_output,
    first_gain,
    first_bias,
    cross_query,
    cross_key,
    cross_value,
    cross_output,
    second_gain,
    second_bias,
    expand_weight,
    reduce_weight,
    third_gain,
    third_bias,
    vision_proj,
):
    image_count = patches.shape[0]
    box = box_columns(box_mask[0], PATCH_ROWS)
    patch_count = patches.shape[1]
    flat_patches = jnp.pad(patches, ((0, 0), (0, PATCH_ROWS - patch_count), (0, 0))).reshape(
        image_count * PATCH_ROWS, patches.shape[2]
    )

    def by_image(values):
        return values.reshape(image_count, PATCH_ROWS, values.shape[-1])

    projected = matmul(flat_patches, vision_proj).astype(jnp.bfloat16)
    own_keys = matmul(projected, cross_key).astype(jnp.bfloat16)
    own_values = matmul(projected, cross_value).astype(jnp.bfloat16)
    far_keys, far_values = from_partner((own_keys, own_values), "mod", 0)
    query_s = matmul(text_tokens, self_query).astype(jnp.bfloat16)
    key_s = matmul(text_tokens, self_key).astype(jnp.bfloat16)
    value_s = matmul(text_tokens, self_value).astype(jnp.bfloat16)
    attended_b, self_log = attend((lengths,), query_s, key_s, value_s, None)
    first_sum = text_tokens.astype(jnp.float32) + matmul(attended_b, self_output)
    normed_one, first_back = jax.vjp(norm_rows, first_sum, first_gain, first_bias)
    normed_one_b = normed_one.astype(jnp.bfloat16)
    query_c = matmul(normed_one_b, cross_query).astype(jnp.bfloat16)
    far_keys, far_values = by_image(far_keys), by_image(far_values)
    crossed_b, cross_log = attend((lengths, row_image), query_c, far_keys, far_values, box)
    second_sum = normed_one + matmul(crossed_b, cross_output)
    normed_two, second_back = jax.vjp(norm_rows, second_sum, second_gain, second_bias)
    normed_two_b = normed_two.astype(jnp.bfloat16)
    hidden = matmul(normed_two_b, expand_weight)
    activated, gelu_back = jax.vjp(gelu_exact, hidden)
    activated_b = activated.astype(jnp.bfloat16)
    third_sum = normed_two + matmul(activated_b, reduce_weight)
    normed_three, third_back = jax.vjp(norm_rows, third_sum, third_gain, third_bias)
    merged = normed_three.astype(jnp.bfloat16)
    grad_third, grad_third_gain, grad_third_bias = third_back(cotangent.astype(jnp.float32))
    grad_third_b = grad_third.astype(jnp.bfloat16)
    grad_reduce = matmul_left_t(activated_b, grad_third_b)
    grad_active = matmul_right_t(grad_third_b, reduce_weight)
    grad_hidden = gelu_back(grad_active)[0].astype(jnp.bfloat16)
    grad_expand = matmul_left_t(normed_two_b, grad_hidden)
    grad_normed_two = grad_third + matmul_right_t(grad_hidden, expand_weight)
    grad_second, grad_second_gain, grad_second_bias = second_back(grad_normed_two)
    grad_second_b = grad_second.astype(jnp.bfloat16)
    grad_cross_output = matmul_left_t(crossed_b, grad_second_b)
    grad_crossed = matmul_right_t(grad_second_b, cross_output).astype(jnp.bfloat16)
    grad_query_c, grad_far_keys, grad_far_values = attend_back(
        (lengths, row_image), query_c, far_keys, far_values, grad_crossed, cross_log, box
    )
    grad_far_keys = grad_far_keys.reshape(projected.shape)
    grad_far_values = grad_far_values.reshape(projected.shape)
    grad_cross_query = matmul_left_t(normed_one_b, grad_query_c)
    grad_normed_one = grad_second + matmul_right_t(grad_query_c, cross_query)
    grad_first, grad_first_gain, grad_first_bias = first_back(grad_normed_one)
    grad_first_b = grad_first.astype(jnp.bfloat16)
    grad_self_output = matmul_left_t(attended_b, grad_first_b)
    grad_attended = matmul_right_t(grad_first_b, self_output).astype(jnp.bfloat16)
    grad_query_s, grad_key_s, grad_value_s = attend_back(
        (lengths,), query_s, key_s, value_s, grad_attended, self_log, None
    )
    grad_self_query = matmul_left_t(text_tokens, grad_query_s)
    grad_self_key = matmul_left_t(text_tokens, grad_key_s)
    grad_self_value = matmul_left_t(text_tokens, grad_value_s)
    text_grad = (
        grad_first
        + matmul_right_t(grad_query_s, self_query)
        + matmul_right_t(grad_key_s, self_key)
        + matmul_right_t(grad_value_s, self_value)
    )
    back_keys, back_values = from_partner((grad_far_keys, grad_far_values), "mod", 0)
    grad_cross_key = matmul_left_t(projected, back_keys)
    grad_cross_value = matmul_left_t(projected, back_values)
    grad_projected = (
        matmul_right_t(back_keys, cross_key) + matmul_right_t(back_values, cross_value)
    ).astype(jnp.bfloat16)
    grad_vision = matmul_left_t(flat_patches, grad_projected)
    patch_grad = by_image(matmul_right_t(grad_projected, vision_proj))[:, :patch_count]
    one_way, other_way = stage_orders()
    half_ff = grad_reduce.shape[0] // 2
    sum_reduce = jnp.concatenate(
        [total(grad_reduce[:half_ff], one_way), total(grad_reduce[half_ff:], other_way)], axis=0
    )
    sum_expand = jnp.concatenate(
        [total(grad_expand[:, :half_ff], one_way), total(grad_expand[:, half_ff:], other_way)],
        axis=1,
    )
    width = grad_cross_query.shape[1]

    def couple(left, right, order):
        both = total(jnp.concatenate([left, right], axis=1), order)
        return both[:, :width], both[:, width:]

    sum_cross_output, sum_cross_query = couple(grad_cross_output, grad_cross_query, one_way)
    sum_cross_key, sum_cross_value = couple(grad_cross_key, grad_cross_value, other_way)
    sum_vision = total(grad_vision, one_way)
    sum_self_output, sum_self_query = couple(grad_self_output, grad_self_query, other_way)
    sum_self_key, sum_self_value = couple(grad_self_key, grad_self_value, one_way)
    small = sum_everywhere(
        jnp.stack(
            [
                grad_first_gain,
                grad_first_bias,
                grad_second_gain,
                grad_second_bias,
                grad_third_gain,
                grad_third_bias,
            ]
        )
    )
    return (
        merged,
        text_grad,
        patch_grad,
        sum_self_query,
        sum_self_key,
        sum_self_value,
        sum_self_output,
        small[0],
        small[1],
        sum_cross_query,
        sum_cross_key,
        sum_cross_value,
        sum_cross_output,
        small[2],
        small[3],
        sum_expand,
        sum_reduce,
        small[4],
        small[5],
        sum_vision,
    )


def solution(mesh):
    placed = (
        P(("mod", "dp"), None),
        P(("mod", "dp"), None, None),
        P(("mod", "dp"), None),
        P(("mod", "dp"), None),
        P(("mod", "dp"), None, None),
        P(("mod", "dp"), None),
        P(),
        P(),
        P(),
        P(),
        P(),
        P(),
        P(),
        P(),
        P(),
        P(),
        P(),
        P(),
        P(),
        P(),
        P(),
        P(),
        P(),
    )
    return jax.shard_map(
        on_device,
        mesh=mesh,
        in_specs=placed,
        out_specs=(
            P(("mod", "dp"), None),
            P(("mod", "dp"), None),
            P(("mod", "dp"), None, None),
            P(),
            P(),
            P(),
            P(),
            P(),
            P(),
            P(),
            P(),
            P(),
            P(),
            P(),
            P(),
            P(),
            P(),
            P(),
            P(),
            P(),
        ),
        check_vma=False,
    )
```

```python
import functools

import jax
import jax.numpy as jnp
from jax import lax
from jax.experimental import pallas as pl
from jax.experimental.pallas import tpu as pltpu
from jax.sharding import PartitionSpec as P

HEAD_DIM = 64
TOK_DEV = 768
PATCH_ROWS = 160
FF_TILE = 768
ROW_TILE = 128
OUT_TILE = 768
LONGEST = 40
WINDOW = 64
SLOTS = 128
LANES = 256
BASES = (0, 128, 384, 512)
TOGETHER = 4
TAKES = {
    "self_attend": 8,
    "cross_attend": 9,
    "feed_forward": 17,
    "feed_back": 15,
    "cross_attend_back": 21,
    "self_attend_back": 13,
    "first_back": 5,
    "text_back": 4,
    "patch_back": 5,
    "reduce_terms": 5,
    "expand_terms": 8,
    "cross_terms": 10,
}


def cost(name):
    return pl.CostEstimate(
        flops=TAKES.get(name, 4) * 1_100_000_000, bytes_accessed=1 << 16, transcendentals=0
    )


def norm_rows(values, gain_row, shift_row):
    centred = values - jnp.mean(values, axis=-1, keepdims=True)
    spread = jnp.mean(centred * centred, axis=-1, keepdims=True)
    return centred * lax.rsqrt(spread + 1e-05) * gain_row + shift_row


def matmul(left, right):
    return jnp.dot(left, right, preferred_element_type=jnp.float32)


def norm_rows(values, gain_row, shift_row):
    centred = values - jnp.mean(values, axis=-1, keepdims=True)
    spread = jnp.mean(centred * centred, axis=-1, keepdims=True)
    return centred * lax.rsqrt(spread + 1e-05) * gain_row + shift_row


def matmul(left, right):
    return jnp.dot(left, right, preferred_element_type=jnp.float32)


def slot_of(shape, dim):
    slot = lax.broadcasted_iota(jnp.int32, shape, dim)
    part = (slot >= LONGEST).astype(jnp.int32) + (slot >= 2 * LONGEST).astype(jnp.int32)
    return part, slot - part * LONGEST


def fill_head_masks(masks_ref):
    part, _ = slot_of((SLOTS, LANES), 0)
    lane = lax.broadcasted_iota(jnp.int32, (SLOTS, LANES), 1)
    for odd in range(2):
        low = HEAD_DIM * (part + odd)
        inside = (lane >= low) & (lane < low + HEAD_DIM)
        masks_ref[odd] = jnp.where(inside, 1.0, 0.0).astype(jnp.bfloat16)


def row_place(start):
    first = jnp.minimum(lax.bitwise_and(start, -16), TOK_DEV - WINDOW)
    return pl.multiple_of(first, 16), start - first


def pick_rows(offset, length):
    _, place = slot_of((SLOTS, WINDOW), 0)
    at = lax.broadcasted_iota(jnp.int32, (SLOTS, WINDOW), 1)
    return jnp.where((place < length) & (at == place + offset), 1.0, 0.0).astype(jnp.bfloat16)


def put_rows(offset, length):
    _, place = slot_of((WINDOW, SLOTS), 1)
    at = lax.broadcasted_iota(jnp.int32, (WINDOW, SLOTS), 0)
    return jnp.where((place < length) & (at == place + offset), 1.0, 0.0).astype(jnp.bfloat16)


def dot(left, right, over):
    return lax.dot_general(left, right, (over, ((), ())), preferred_element_type=jnp.float32)


NT = ((1,), (1,))
NN = ((1,), (0,))
TN = ((0,), (0,))


def side_by_side(parts):
    first, second, third, fourth = parts
    half = LANES // 2
    return jnp.concatenate(
        [
            first[:, :half],
            first[:, half:] + second[:, :half],
            second[:, half:],
            third[:, :half],
            third[:, half:] + fourth[:, :half],
            fourth[:, half:],
        ],
        axis=1,
    )


def self_allowed(offset, length):
    at = lax.broadcasted_iota(jnp.int32, (WINDOW, SLOTS), 0)
    return (at >= offset) & (at < offset + length)


def cross_allowed(box_ref, row):
    turn = lax.broadcasted_iota(jnp.int32, (SLOTS, SLOTS), 0)
    chosen = jnp.where(turn == row, 1.0, 0.0).astype(jnp.bfloat16)
    return dot(box_ref[...], chosen, NN) > 0.5


def row_keys(cross, first, image, ref, base):
    if cross:
        return ref[image, :, base : base + LANES]
    return ref[pl.ds(first, WINDOW), base : base + LANES]


def forward_kernel(cross, *refs):
    if cross:
        lengths, images, box_ref, q_ref, k_ref, v_ref, out_ref, log_ref, masks, total = refs
    else:
        lengths, q_ref, k_ref, v_ref, out_ref, log_ref, masks, total = refs
        images = box_ref = None
    fill_head_masks(masks)
    total[...] = jnp.zeros_like(total)

    def rows_at_once(step, start):
        work = []
        for turn in range(TOGETHER):
            row = TOGETHER * step + turn
            length = lengths[0, row]
            first, offset = row_place(start)
            work.append((row, length, images[0, row] if cross else None, first, offset))
            start = start + length
        picked = [
            dot(pick_rows(offset, length), q_ref[pl.ds(first, WINDOW), :], NN)
            for _, length, _, first, offset in work
        ]
        picked = [(p * HEAD_DIM ** (-0.5)).astype(jnp.bfloat16) for p in picked]
        allowed = [
            cross_allowed(box_ref, row) if cross else self_allowed(offset, length)
            for row, length, _, _, offset in work
        ]
        each = [(turn, group) for turn in range(TOGETHER) for group in range(len(BASES))]
        scores = {}
        for turn, group in each:
            _, _, image, first, _ = work[turn]
            base = BASES[group]
            queries = picked[turn][:, base : base + LANES] * masks[group % 2]
            keys_in = row_keys(cross, first, image, k_ref, base)
            scores[turn, group] = dot(keys_in, queries, NT)
        soft = {}
        for turn, group in each:
            row = work[turn][0]
            masked = jnp.where(allowed[turn], scores[turn, group], -1e30)
            top = jnp.max(masked, axis=0, keepdims=True)
            exps = jnp.exp(masked - top)
            summed = jnp.sum(exps, axis=0, keepdims=True)
            soft[turn, group] = (exps * (1.0 / summed)).astype(jnp.bfloat16)
            log_ref[row, group : group + 1, :] = top + jnp.log(summed)
        mixed = {}
        for turn, group in each:
            _, _, image, first, _ = work[turn]
            values_in = row_keys(cross, first, image, v_ref, BASES[group])
            mixed[turn, group] = (
                dot(soft[turn, group], values_in, TN).astype(jnp.bfloat16) * masks[group % 2]
            )
        for turn in range(TOGETHER):
            _, length, _, first, offset = work[turn]
            side = side_by_side([mixed[turn, group] for group in range(len(BASES))])
            total[pl.ds(first, WINDOW), :] += dot(put_rows(offset, length), side, NN)
        return start

    rows = lengths.shape[1]
    lax.fori_loop(0, rows // TOGETHER, rows_at_once, jnp.int32(0))
    out_ref[...] = total[...].astype(out_ref.dtype)


def backward_kernel(cross, *refs):
    if cross:
        lengths, images, box_ref, key_ref, value_ref = refs[:5]
        refs = refs[5:]
        far_ref, refs = refs[8], refs[:8] + refs[9:]
    else:
        lengths, refs = refs[0], refs[1:]
        images = box_ref = None
    q_ref, k_ref, v_ref, g_ref, log_ref, dq_ref, dk_ref, dv_ref, masks, dq, dk, dv = refs
    fill_head_masks(masks)
    dq[...] = jnp.zeros_like(dq)
    dk[...] = jnp.zeros_like(dk)
    dv[...] = jnp.zeros_like(dv)

    def rows_at_once(step, start):
        work = []
        for turn in range(TOGETHER):
            row = TOGETHER * step + turn
            length = lengths[0, row]
            first, offset = row_place(start)
            work.append((row, length, images[0, row] if cross else None, first, offset))
            start = start + length
        picks = [pick_rows(offset, length) for _, length, _, _, offset in work]
        picked = [
            (dot(pick, q_ref[pl.ds(w[3], WINDOW), :], NN) * HEAD_DIM ** (-0.5)).astype(jnp.bfloat16)
            for pick, w in zip(picks, work)
        ]
        picked_g = [
            dot(pick, g_ref[pl.ds(w[3], WINDOW), :], NN).astype(jnp.bfloat16)
            for pick, w in zip(picks, work)
        ]
        allowed = [
            cross_allowed(box_ref, row) if cross else self_allowed(offset, length)
            for row, length, _, _, offset in work
        ]
        each = [(turn, group) for turn in range(TOGETHER) for group in range(len(BASES))]
        queries, grads, scores, grad_soft = {}, {}, {}, {}
        for turn, group in each:
            _, _, image, first, _ = work[turn]
            base = BASES[group]
            mask = masks[group % 2]
            queries[turn, group] = picked[turn][:, base : base + LANES] * mask
            grads[turn, group] = picked_g[turn][:, base : base + LANES] * mask
            keys_in = row_keys(cross, first, image, k_ref, base)
            values_in = row_keys(cross, first, image, v_ref, base)
            scores[turn, group] = dot(keys_in, queries[turn, group], NT)
            grad_soft[turn, group] = dot(values_in, grads[turn, group], NT)
        soft, grad_scores = {}, {}
        for turn, group in each:
            row = work[turn][0]
            masked = jnp.where(allowed[turn], scores[turn, group], -1e30)
            kept = jnp.exp(masked - log_ref[row, group : group + 1, :])
            inner = jnp.sum(kept * grad_soft[turn, group], axis=0, keepdims=True)
            grad_scores[turn, group] = (kept * (grad_soft[turn, group] - inner)).astype(
                jnp.bfloat16
            )
            soft[turn, group] = kept.astype(jnp.bfloat16)
        grad_k, grad_v, grad_q = {}, {}, {}
        for turn, group in each:
            _, _, image, first, _ = work[turn]
            keys_in = row_keys(cross, first, image, k_ref, BASES[group])
            grad_k[turn, group] = dot(grad_scores[turn, group], queries[turn, group], NN)
            grad_v[turn, group] = dot(soft[turn, group], grads[turn, group], NN)
            grad_q[turn, group] = (
                dot(grad_scores[turn, group], keys_in, TN) * HEAD_DIM ** (-0.5)
            ).astype(jnp.bfloat16) * masks[group % 2]
        for turn in range(TOGETHER):
            _, length, image, first, offset = work[turn]
            every = range(len(BASES))
            side_k = side_by_side([grad_k[turn, group] for group in every])
            side_v = side_by_side([grad_v[turn, group] for group in every])
            side_q = side_by_side([grad_q[turn, group] for group in every])
            if cross:
                dk[image] += side_k
                dv[image] += side_v
            else:
                dk[pl.ds(first, WINDOW), :] += side_k
                dv[pl.ds(first, WINDOW), :] += side_v
            dq[pl.ds(first, WINDOW), :] += dot(put_rows(offset, length), side_q, NN)
        return start

    rows = lengths.shape[1]
    lax.fori_loop(0, rows // TOGETHER, rows_at_once, jnp.int32(0))
    dq_ref[...] = dq[...].astype(dq_ref.dtype)
    dk_ref[...] = dk[...].astype(dk_ref.dtype)
    dv_ref[...] = dv[...].astype(dv_ref.dtype)
    if cross:

        def project(image, _):
            projected = dot(dk_ref[image], key_ref[...], NT) + dot(dv_ref[image], value_ref[...], NT)
            far_ref[image] = projected.astype(far_ref.dtype)
            return _

        lax.fori_loop(0, k_ref.shape[0], project, 0)


def in_smem():
    return pl.BlockSpec(memory_space=pltpu.SMEM)


def in_vmem():
    return pl.BlockSpec(memory_space=pltpu.VMEM)


def attend(scalars, queries, keys_in, values_in, box):
    cross = box is not None
    rows = scalars[0].shape[1]
    tensors = ((box,) if cross else ()) + (queries, keys_in, values_in)
    return pl.pallas_call(
        functools.partial(forward_kernel, cross),
        out_shape=(
            jax.ShapeDtypeStruct(queries.shape, jnp.bfloat16),
            jax.ShapeDtypeStruct((rows, len(BASES), SLOTS), jnp.float32),
        ),
        in_specs=[in_smem()] * len(scalars) + [in_vmem()] * len(tensors),
        out_specs=(in_vmem(), in_vmem()),
        scratch_shapes=[
            pltpu.VMEM((2, SLOTS, LANES), jnp.bfloat16),
            pltpu.VMEM(queries.shape, jnp.float32),
        ],
        compiler_params=pltpu.CompilerParams(vmem_limit_bytes=24 << 20),
        cost_estimate=cost("cross_attend" if cross else "self_attend"),
        name="cross_attend" if cross else "self_attend",
    )(*scalars, *tensors)


def attend_back(scalars, queries, keys_in, values_in, grads, logs, extra=()):
    cross = bool(extra)
    tensors = extra + (queries, keys_in, values_in, grads, logs)
    results = (queries, keys_in, values_in) + ((keys_in,) if cross else ())
    return pl.pallas_call(
        functools.partial(backward_kernel, cross),
        out_shape=tuple(jax.ShapeDtypeStruct(a.shape, jnp.bfloat16) for a in results),
        in_specs=[in_smem()] * len(scalars) + [in_vmem()] * len(tensors),
        out_specs=(in_vmem(),) * len(results),
        scratch_shapes=[
            pltpu.VMEM((2, SLOTS, LANES), jnp.bfloat16),
            pltpu.VMEM(queries.shape, jnp.float32),
            pltpu.VMEM(keys_in.shape, jnp.float32),
            pltpu.VMEM(keys_in.shape, jnp.float32),
        ],
        compiler_params=pltpu.CompilerParams(vmem_limit_bytes=28 << 20),
        cost_estimate=cost("cross_attend_back" if cross else "self_attend_back"),
        name="cross_attend_back" if cross else "self_attend_back",
    )(*scalars, *tensors)


def phi_parts(values):
    size = jnp.abs(values)
    tail = jnp.exp(-0.5 * values * values)
    turn = 1.0 / (1.0 + (0.3275911 * 0.5**0.5) * size)
    series = 1.061405429 * turn - 1.453152027
    series = series * turn + 1.421413741
    series = series * turn - 0.284496736
    series = series * turn + 0.254829592
    half = (0.5 * turn) * series * tail
    return jnp.where(values >= 0, 1.0 - half, half), tail * 0.3989422804014327


def centre(values):
    off = values - jnp.mean(values, axis=-1, keepdims=True)
    scale = lax.rsqrt(jnp.mean(off * off, axis=-1, keepdims=True) + 1e-05)
    return off * scale, scale


def centre_back(grads, normed, scale, gain):
    inner = grads * gain
    mean = jnp.mean(inner, axis=-1, keepdims=True)
    along = jnp.mean(inner * normed, axis=-1, keepdims=True)
    return scale * (inner - mean - normed * along)


def total_rows(values):
    return jnp.sum(values, axis=0, keepdims=True)


def feed_forward_kernel(
    x_ref, xb_ref, expand_ref, reduce_ref, cot_ref, gain_ref, shift_ref,
    active_ref, slope_ref, merged_ref, third_ref, third_b_ref, dgain_ref, dshift_ref, held, acc,
):
    tokens, width = x_ref.shape
    inner = expand_ref.shape[1]
    tiles = inner // FF_TILE

    def hide(tile, slot):
        lanes = pl.ds(pl.multiple_of(tile * FF_TILE, FF_TILE), FF_TILE)
        held[slot] = dot(xb_ref[...], expand_ref[:, lanes], NN)

    def activate(tile, slot):
        lanes = pl.ds(pl.multiple_of(tile * FF_TILE, FF_TILE), FF_TILE)
        hidden = held[slot]
        share, density = phi_parts(hidden)
        active_ref[:, lanes] = (hidden * share).astype(jnp.bfloat16)
        slope_ref[:, lanes] = (share + hidden * density).astype(jnp.bfloat16)

    hide(0, 0)

    def both(pair, _):
        for slot in range(2):
            tile = 2 * pair + slot
            hide(tile + 1, 1 - slot)
            activate(tile, slot)
        return _

    lax.fori_loop(0, tiles // 2 - 1, both, 0)
    hide(tiles - 1, 1)
    activate(tiles - 2, 0)
    activate(tiles - 1, 1)

    def project(tile, _):
        lanes = pl.ds(pl.multiple_of(tile * OUT_TILE, OUT_TILE), OUT_TILE)
        acc[:, lanes] = x_ref[:, lanes] + dot(active_ref[...], reduce_ref[:, lanes], NN)
        return _

    lax.fori_loop(0, width // OUT_TILE, project, 0)
    dgain_ref[...] = jnp.zeros_like(dgain_ref)
    dshift_ref[...] = jnp.zeros_like(dshift_ref)

    def finish(part, _):
        rows = pl.ds(pl.multiple_of(part * ROW_TILE, ROW_TILE), ROW_TILE)
        normed, scale = centre(acc[rows, :])
        merged_ref[rows, :] = (normed * gain_ref[...] + shift_ref[...]).astype(jnp.bfloat16)
        grads = cot_ref[rows, :].astype(jnp.float32)
        third = centre_back(grads, normed, scale, gain_ref[...])
        third_ref[rows, :] = third
        third_b_ref[rows, :] = third.astype(jnp.bfloat16)
        dgain_ref[...] += total_rows(grads * normed)
        dshift_ref[...] += total_rows(grads)
        return _

    lax.fori_loop(0, tokens // ROW_TILE, finish, 0)


def feed_forward(x, xb, expand, reduce, cot, gain, shift):
    tokens, width = x.shape
    inner = expand.shape[1]
    wide = lambda dtype: jax.ShapeDtypeStruct((tokens, inner), dtype)
    square = lambda dtype: jax.ShapeDtypeStruct((tokens, width), dtype)
    flat = jax.ShapeDtypeStruct((1, width), jnp.float32)
    return pl.pallas_call(
        feed_forward_kernel,
        in_specs=[in_vmem()] * 7,
        out_specs=(in_vmem(),) * 7,
        out_shape=(
            wide(jnp.bfloat16), wide(jnp.bfloat16), square(jnp.bfloat16),
            square(jnp.float32), square(jnp.bfloat16), flat, flat,
        ),
        scratch_shapes=[
            pltpu.VMEM((2, tokens, FF_TILE), jnp.float32), pltpu.VMEM((tokens, width), jnp.float32)
        ],
        compiler_params=pltpu.CompilerParams(vmem_limit_bytes=24 << 20),
        cost_estimate=cost("feed_forward"),
        name="feed_forward",
    )(x, xb, expand, reduce, cot, gain[None], shift[None])


def feed_back_kernel(
    third_ref, third_b_ref, slope_ref, expand_ref, reduce_ref, second_ref, gain_ref, cross_out_ref,
    hidden_ref, grad_ref, grad_b_ref, crossed_ref, dgain_ref, dshift_ref, acc,
):
    step = pl.program_id(0)
    active = dot(third_b_ref[...], reduce_ref[...], NT)
    hidden = (active * slope_ref[...].astype(jnp.float32)).astype(jnp.bfloat16)
    hidden_ref[...] = hidden
    part = dot(hidden, expand_ref[...], NT)

    @pl.when(step == 0)
    def _():
        acc[...] = third_ref[...] + part

    @pl.when(step > 0)
    def _():
        acc[...] += part

    @pl.when(step == pl.num_programs(0) - 1)
    def _():
        norm_back(acc, second_ref, gain_ref, grad_ref, grad_b_ref, dgain_ref, dshift_ref)
        crossed_ref[...] = dot(grad_b_ref[...], cross_out_ref[...], NT).astype(jnp.bfloat16)


def norm_back(upstream, summed_ref, gain_ref, grad_ref, grad_b_ref, dgain_ref, dshift_ref):
    dgain_ref[...] = jnp.zeros_like(dgain_ref)
    dshift_ref[...] = jnp.zeros_like(dshift_ref)

    def some_rows(part, _):
        rows = pl.ds(pl.multiple_of(part * ROW_TILE, ROW_TILE), ROW_TILE)
        normed, scale = centre(summed_ref[rows, :])
        grads = upstream[rows, :]
        grad = centre_back(grads, normed, scale, gain_ref[...])
        grad_ref[rows, :] = grad
        grad_b_ref[rows, :] = grad.astype(jnp.bfloat16)
        dgain_ref[...] += total_rows(grads * normed)
        dshift_ref[...] += total_rows(grads)
        return _

    lax.fori_loop(0, summed_ref.shape[0] // ROW_TILE, some_rows, 0)


def feed_back(third, third_b, slope, expand, reduce, second_sum, gain, cross_out):
    tokens, width = third.shape
    inner = expand.shape[1]
    square = lambda dtype: jax.ShapeDtypeStruct((tokens, width), dtype)
    flat = jax.ShapeDtypeStruct((1, width), jnp.float32)
    tile = pl.BlockSpec((tokens, FF_TILE), lambda i: (0, i))
    return pl.pallas_call(
        feed_back_kernel,
        grid=(inner // FF_TILE,),
        in_specs=[
            in_vmem(),
            in_vmem(),
            tile,
            pl.BlockSpec((width, FF_TILE), lambda i: (0, i)),
            pl.BlockSpec((FF_TILE, width), lambda i: (i, 0)),
            in_vmem(),
            in_vmem(),
            in_vmem(),
        ],
        out_specs=(tile,) + (in_vmem(),) * 5,
        out_shape=(
            jax.ShapeDtypeStruct((tokens, inner), jnp.bfloat16), square(jnp.float32),
            square(jnp.bfloat16), square(jnp.bfloat16), flat, flat,
        ),
        scratch_shapes=[pltpu.VMEM((tokens, width), jnp.float32)],
        compiler_params=pltpu.CompilerParams(vmem_limit_bytes=36 << 20),
        cost_estimate=cost("feed_back"),
        name="feed_back",
    )(third, third_b, slope, expand, reduce, second_sum, gain[None], cross_out)


def first_back_kernel(
    gq_ref, query_ref, second_ref, first_ref, gain_ref, output_ref,
    grad_ref, grad_b_ref, attended_ref, dgain_ref, dshift_ref, acc,
):
    acc[...] = second_ref[...] + dot(gq_ref[...], query_ref[...], NT)
    norm_back(acc, first_ref, gain_ref, grad_ref, grad_b_ref, dgain_ref, dshift_ref)
    attended_ref[...] = dot(grad_b_ref[...], output_ref[...], NT).astype(jnp.bfloat16)


def first_back(grad_query, cross_query, grad_second, first_sum, gain, self_output):
    square = lambda dtype: jax.ShapeDtypeStruct(first_sum.shape, dtype)
    flat = jax.ShapeDtypeStruct((1, first_sum.shape[1]), jnp.float32)
    return plain_call(
        first_back_kernel,
        (square(jnp.float32), square(jnp.bfloat16), square(jnp.bfloat16), flat, flat),
        (grad_query, cross_query, grad_second, first_sum, gain[None], self_output),
        [pltpu.VMEM(first_sum.shape, jnp.float32)],
        "first_back",
    )


def plain_call(kernel, out_shape, arrays, scratch, name, scalars=()):
    return pl.pallas_call(
        kernel,
        out_shape=out_shape,
        in_specs=[in_smem()] * len(scalars) + [in_vmem()] * len(arrays),
        out_specs=jax.tree.map(lambda _: in_vmem(), out_shape),
        scratch_shapes=scratch,
        compiler_params=pltpu.CompilerParams(vmem_limit_bytes=24 << 20),
        cost_estimate=cost(name),
        name=name,
    )(*scalars, *arrays)


def text_back_kernel(first_ref, *refs):
    out_ref = refs[-1]
    out_ref[...] = first_ref[...]
    for grad_ref, weight_ref in zip(refs[:3], refs[3:6]):
        out_ref[...] += dot(grad_ref[...], weight_ref[...], NT)


def text_back(grad_first, grads, weights):
    shape = jax.ShapeDtypeStruct(grad_first.shape, jnp.float32)
    return plain_call(text_back_kernel, shape, (grad_first, *grads, *weights), [], "text_back")


def patch_back_kernel(grad_ref, weight_ref, out_ref):
    for image in range(out_ref.shape[0]):
        rows = grad_ref[image * PATCH_ROWS : (image + 1) * PATCH_ROWS]
        out_ref[image] = dot(rows, weight_ref[...], NT)[: out_ref.shape[1]]


def patch_back(grad_projected, vision_proj, shape):
    return plain_call(
        patch_back_kernel,
        jax.ShapeDtypeStruct(shape, jnp.float32),
        (grad_projected, vision_proj),
        [],
        "patch_back",
    )


def terms_of(pieces, arrays, shape, name, turned=None):
    def kernel(core_ref, *refs):
        keep, away = refs[len(arrays) : len(arrays) + 2]
        scratch = refs[len(arrays) + 2 :]

        def put(half, shards, rows, columns, product):
            values = product.astype(jnp.bfloat16)
            values = values.reshape((-1, values.shape[0] // 16 if shards is None else shards[1], values.shape[1]))
            first = slice(None) if shards is None else shards[0]

            def store(ref):
                ref[first, rows, columns] = values

            pl.when(core_ref[0] == half)(lambda: store(keep))
            pl.when(core_ref[0] != half)(lambda: store(away))

        pieces(refs[: len(arrays)], scratch, put)

    out = jax.ShapeDtypeStruct(shape, jnp.bfloat16)
    scratch = [] if turned is None else [pltpu.VMEM(turned, jnp.bfloat16)]
    return plain_call(kernel, (out, out), arrays, scratch, name, (my_bit(*CORE)[None],))


def reduce_terms(refs, scratch, put):
    active, grads = refs
    blocks = active.shape[1] // FF_TILE
    rows = active.shape[1] // 16
    held = 16 // blocks

    def block(at, _):
        lanes = pl.ds(pl.multiple_of(at * FF_TILE, FF_TILE), FF_TILE)
        product = dot(active[:, lanes], grads[...], TN)
        half = product.shape[1] // 2
        shards = (pl.ds(at * held, held), rows)
        put(0, shards, slice(None), slice(None), product[:, :half])
        put(1, shards, slice(None), slice(None), product[:, half:])
        return _

    lax.fori_loop(0, blocks, block, 0)


def expand_terms(refs, scratch, put):
    values, grads = refs
    (turned,) = scratch
    turned[...] = values[...].T
    blocks = grads.shape[1] // FF_TILE

    for at in range(blocks):
        product = dot(turned[...], grads[:, at * FF_TILE : (at + 1) * FF_TILE], NN)
        place = at % (blocks // 2)
        columns = slice(place * FF_TILE, (place + 1) * FF_TILE)
        put(at // (blocks // 2), None, slice(None), columns, product)


def cross_terms(refs, scratch, put):
    crossed, grad_second, normed_one, grad_query, far, grad_key, grad_value = refs
    width = crossed.shape[1]
    left, right = slice(0, width), slice(width, 2 * width)
    put(0, None, slice(None), left, dot(crossed[...], grad_second[...], TN))
    put(0, None, slice(None), right, dot(normed_one[...], grad_query[...], TN))
    put(1, None, slice(None), left, dot(far[...], grad_key[...], TN))
    put(1, None, slice(None), right, dot(far[...], grad_value[...], TN))


def pair_terms(refs, scratch, put):
    left, left_grad, right, right_grad = refs
    every = slice(None)
    put(0, None, every, every, dot(left[...], left_grad[...], TN))
    put(1, None, every, every, dot(right[...], right_grad[...], TN))


def vision_terms(refs, scratch, put):
    patches, grads = refs
    half = patches.shape[1] // 2
    every = slice(None)
    put(0, None, every, every, dot(patches[:, :half], grads[...], TN))
    put(1, None, every, every, dot(patches[:, half:], grads[...], TN))


def box_columns(box_mask, patch_rows):
    turned = jnp.transpose(box_mask).astype(jnp.bfloat16)
    return jnp.pad(
        turned, ((0, patch_rows - turned.shape[0]), (0, SLOTS - turned.shape[1]))
    )


def flip_bit(values, axis, bit):
    count = lax.axis_size(axis)
    return lax.ppermute(values, axis, [(i, i ^ (1 << bit)) for i in range(count)])


def my_bit(axis, bit):
    return (lax.axis_index(axis) >> bit) & 1


def stage_order(names):
    bits = {"x": [("dp", 1)], "y": [("mod", 0)], "z": [("dp", 2), ("dp", 3)]}
    return sum([bits[name] for name in names], [])


def other_bits():
    dp_bits = lax.axis_size("dp").bit_length() - 1
    mod_bits = lax.axis_size("mod").bit_length() - 1
    return [("mod", bit) for bit in range(1, mod_bits)] + [("dp", bit) for bit in range(4, dp_bits)]


CORE = ("dp", 0)
ORDERS = {"r": "yxz", "e": "zxy", "c": "xyz", "s": "yxz", "q": "yxz", "v": "xyz"}
TURNS = "PergAvcrTvscvgerqvcesvrcgvesqvcesvrcseqvsVqsqcsrqeqsRSqceCqEQ"


def place_in(order):
    place = jnp.int32(0)
    for axis, bit in order:
        place = 2 * place + my_bit(axis, bit)
    return place


class Sum:
    def __init__(self, keep, away, order):
        self.order = order = stage_order(order)
        self.kept = keep
        self.flown = flip_bit(away, *CORE)
        self.steps = [("scatter", stage) for stage in order]
        self.steps += [("add", stage) for stage in other_bits()]
        self.steps += [("gather", stage) for stage in reversed(order)] + [("last", CORE)]
        self.before = "add"

    def advance(self):
        if self.before == "add":
            values = self.kept + self.flown
        else:
            values = jnp.concatenate([self.kept, self.flown], axis=0)
        kind, (axis, bit) = self.steps.pop(0)
        if kind == "scatter":
            mine = my_bit(axis, bit)
            pair = values.reshape((2, values.shape[0] // 2) + values.shape[1:])
            away = lax.dynamic_index_in_dim(pair, 1 - mine, 0, False)
            self.kept = lax.dynamic_index_in_dim(pair, mine, 0, False)
        else:
            self.kept = away = values
        self.flown = flip_bit(away, axis, bit)
        self.before = "add" if kind in ("scatter", "add") else "gather"


class Line:
    def __init__(self):
        self.token = jnp.zeros((1, 1), jnp.float32)

    def meet(self, values, *sums):
        flown = [one.flown for one in sums]
        values, self.token, flown = lax.optimization_barrier((values, self.token, flown))
        for one, arrived in zip(sums, flown):
            one.flown = arrived
            if one.steps:
                one.advance()
        return values


class SmallSum:
    def __init__(self, values):
        self.steps = [CORE] + stage_order("xyz") + other_bits()
        self.kept = values
        self.flown = jnp.zeros_like(values)
        self.advance()

    def advance(self):
        self.kept = self.kept + self.flown
        self.flown = flip_bit(self.kept, *self.steps.pop(0))

    @property
    def total(self):
        return self.kept + self.flown


def spread(one, shapes, fill, name):
    own, other = one.kept, one.flown
    shards, rows, columns = own.shape
    at = jnp.stack([my_bit(*CORE), place_in(one.order)])

    def kernel(at_ref, own_ref, other_ref, *outs):
        inner = at_ref[1] & 3

        def write(low, high):
            for step in range(4):
                fill(low.at[step ^ inner], high.at[step ^ inner], outs, step)

        pl.when(at_ref[0] == 0)(lambda: write(own_ref, other_ref))
        pl.when(at_ref[0] == 1)(lambda: write(other_ref, own_ref))

    def block_of(shape):
        lead = len(shape) - 3
        return pl.BlockSpec(
            shape[:lead] + (4,) + shape[lead + 1 :],
            lambda i, at_ref: (0,) * lead + (i, 0, 0),
        )

    taken = pl.BlockSpec((4, rows, columns), lambda i, at_ref: (i ^ (at_ref[1] >> 2), 0, 0))
    return pl.pallas_call(
        kernel,
        out_shape=tuple(jax.ShapeDtypeStruct(shape, jnp.float32) for shape in shapes),
        grid_spec=pltpu.PrefetchScalarGridSpec(
            num_scalar_prefetch=1,
            grid=(shards // 4,),
            in_specs=[taken, taken],
            out_specs=tuple(block_of(shape) for shape in shapes),
        ),
        compiler_params=pltpu.CompilerParams(vmem_limit_bytes=24 << 20),
        cost_estimate=pl.CostEstimate(
            flops=0, bytes_accessed=12 * own.size, transcendentals=0
        ),
        name=name,
    )(at, own, other)


def fill_columns(low, high, outs, step):
    columns = low.shape[-1]
    outs[0][step, :, :columns] = low[...].astype(jnp.float32)
    outs[0][step, :, columns:] = high[...].astype(jnp.float32)


def fill_couples(low, high, outs, step):
    columns = low.shape[-1] // 2
    for half, taken in enumerate((low, high)):
        outs[2 * half][step] = taken[:, :columns].astype(jnp.float32)
        outs[2 * half + 1][step] = taken[:, columns:].astype(jnp.float32)


def fill_each(low, high, outs, step):
    outs[0][step] = low[...].astype(jnp.float32)
    outs[1][step] = high[...].astype(jnp.float32)


def fill_halves(low, high, outs, step):
    outs[0][0, step] = low[...].astype(jnp.float32)
    outs[0][1, step] = high[...].astype(jnp.float32)


def on_device(
    text_tokens,
    patches,
    lengths,
    row_image,
    box_mask,
    cotangent,
    self_query,
    self_key,
    self_value,
    self_output,
    first_gain,
    first_bias,
    cross_query,
    cross_key,
    cross_value,
    cross_output,
    second_gain,
    second_bias,
    expand_weight,
    reduce_weight,
    third_gain,
    third_bias,
    vision_proj,
):
    image_count = patches.shape[0]
    box = box_columns(box_mask[0], PATCH_ROWS)
    patch_count = patches.shape[1]
    flat_patches = jnp.pad(patches, ((0, 0), (0, PATCH_ROWS - patch_count), (0, 0))).reshape(
        image_count * PATCH_ROWS, patches.shape[2]
    )

    def by_image(values):
        return values.reshape(image_count, PATCH_ROWS, values.shape[-1])

    projected = matmul(flat_patches, vision_proj).astype(jnp.bfloat16)
    far_projected = flip_bit(projected, "mod", 0)
    query_s = matmul(text_tokens, self_query).astype(jnp.bfloat16)
    key_s = matmul(text_tokens, self_key).astype(jnp.bfloat16)
    value_s = matmul(text_tokens, self_value).astype(jnp.bfloat16)
    attended_b, self_log = attend((lengths,), query_s, key_s, value_s, None)
    first_sum = text_tokens.astype(jnp.float32) + matmul(attended_b, self_output)
    normed_one = norm_rows(first_sum, first_gain, first_bias)
    normed_one_b = normed_one.astype(jnp.bfloat16)
    query_c = matmul(normed_one_b, cross_query).astype(jnp.bfloat16)
    far_keys = by_image(matmul(far_projected, cross_key).astype(jnp.bfloat16))
    far_values = by_image(matmul(far_projected, cross_value).astype(jnp.bfloat16))
    crossed_b, cross_log = attend((lengths, row_image), query_c, far_keys, far_values, box)
    second_sum = normed_one + matmul(crossed_b, cross_output)
    normed_two = norm_rows(second_sum, second_gain, second_bias)
    normed_two_b = normed_two.astype(jnp.bfloat16)
    activated_b, slope, merged, grad_third, grad_third_b, grad_third_gain, grad_third_bias = (
        feed_forward(
            normed_two, normed_two_b, expand_weight, reduce_weight, cotangent, third_gain, third_bias
        )
    )
    line = Line()
    width = text_tokens.shape[1]
    inner = expand_weight.shape[1]
    sums = {}
    sums["r"] = Sum(
        *terms_of(
            reduce_terms, (activated_b, grad_third_b), (16, inner // 16, width // 2), "reduce_terms"
        ),
        ORDERS["r"],
    )
    (
        grad_hidden,
        grad_second,
        grad_second_b,
        grad_crossed,
        grad_second_gain,
        grad_second_bias,
    ) = feed_back(
        grad_third,
        grad_third_b,
        slope,
        expand_weight,
        reduce_weight,
        second_sum,
        second_gain,
        cross_output,
    )
    grad_hidden, grad_crossed = line.meet((grad_hidden, grad_crossed), sums["r"])
    sums["e"] = Sum(
        *terms_of(
            expand_terms,
            (normed_two_b, grad_hidden),
            (16, width // 16, inner // 2),
            "expand_terms",
            normed_two_b.shape,
        ),
        ORDERS["e"],
    )
    grad_crossed, sums["e"].kept = line.meet((grad_crossed, sums["e"].kept))
    grads_cross = attend_back(
        (lengths, row_image),
        query_c,
        far_keys,
        far_values,
        grad_crossed,
        cross_log,
        (box, cross_key, cross_value),
    )
    grads_cross = line.meet(grads_cross, sums["e"], sums["r"])
    grad_query_c, grad_far_keys, grad_far_values, grad_far_projected = grads_cross
    grad_far_keys = grad_far_keys.reshape(projected.shape)
    grad_far_values = grad_far_values.reshape(projected.shape)
    grad_projected = flip_bit(grad_far_projected.reshape(projected.shape), "mod", 0)
    grad_first, grad_first_b, grad_attended, grad_first_gain, grad_first_bias = first_back(
        grad_query_c, cross_query, grad_second, first_sum, first_gain, self_output
    )
    small_sum = SmallSum(
        jnp.concatenate(
            [
                grad_first_gain,
                grad_first_bias,
                grad_second_gain,
                grad_second_bias,
                grad_third_gain,
                grad_third_bias,
            ]
        )
    )
    sums["g"] = small_sum
    grad_attended, grad_far_values = line.meet((grad_attended, grad_far_values))
    sums["c"] = Sum(
        *terms_of(
            cross_terms,
            (
                crossed_b,
                grad_second_b,
                normed_one_b,
                grad_query_c,
                far_projected,
                grad_far_keys,
                grad_far_values,
            ),
            (16, width // 16, 2 * width),
            "cross_terms",
        ),
        ORDERS["c"],
    )
    grad_attended = line.meet(grad_attended, sums["r"])
    grad_attended = line.meet(grad_attended, sums["c"], sums["g"])
    patch_grad = patch_back(grad_projected, vision_proj, patches.shape)
    half = vision_proj.shape[0] // 2
    tall = (16, half // 16, width)
    sums["v"] = Sum(
        *terms_of(vision_terms, (flat_patches, grad_projected), tall, "vision_terms"), ORDERS["v"]
    )
    square = (16, width // 16, width)

    def pair_sum(name, order, *arrays):
        return Sum(*terms_of(pair_terms, arrays, square, name), order)

    spreads = {}
    for turn in TURNS:
        if turn == "A":
            grad_attended = line.meet(grad_attended)
            grads_self = attend_back((lengths,), query_s, key_s, value_s, grad_attended, self_log)
            grads_self = line.meet(grads_self)
            grad_query_s, grad_key_s, grad_value_s = grads_self
            sums["s"] = pair_sum(
                "self_terms_one", ORDERS["s"], attended_b, grad_first_b, text_tokens, grad_key_s
            )
            sums["q"] = pair_sum(
                "self_terms_two", ORDERS["q"], text_tokens, grad_query_s, text_tokens, grad_value_s
            )
            text_grad = text_back(grad_first, grads_self, (self_query, self_key, self_value))
        elif turn == "T":
            text_grad = line.meet(text_grad)
        elif turn == "P":
            patch_grad = line.meet(patch_grad)
        elif turn.isupper():
            one = sums[turn.lower()]
            while one.steps:
                line.meet((), one)
            line.meet((), one)
            shapes, fill = {
                "R": ([(16,) + (inner // 16, width)], fill_columns),
                "E": ([(16,) + (width // 16, inner)], fill_columns),
                "C": ([square] * 4, fill_couples),
                "S": ([square] * 2, fill_each),
                "Q": ([square] * 2, fill_each),
                "V": ([(2,) + tall], fill_halves),
            }[turn]
            spreads[turn] = line.meet(spread(one, shapes, fill, "spread_" + turn.lower()))
        else:
            line.meet((), sums[turn])
    while small_sum.steps:
        line.meet((), small_sum)
    small = line.meet(small_sum.total) + line.token
    (sum_reduce,) = spreads["R"]
    (sum_expand,) = spreads["E"]
    sum_cross_output, sum_cross_query, sum_cross_key, sum_cross_value = spreads["C"]
    sum_self_output, sum_self_key = spreads["S"]
    sum_self_query, sum_self_value = spreads["Q"]
    (sum_vision,) = spreads["V"]

    def whole(values, like):
        return values.reshape(like.shape)

    return (
        merged,
        text_grad,
        patch_grad,
        whole(sum_self_query, self_query),
        whole(sum_self_key, self_key),
        whole(sum_self_value, self_value),
        whole(sum_self_output, self_output),
        small[0],
        small[1],
        whole(sum_cross_query, cross_query),
        whole(sum_cross_key, cross_key),
        whole(sum_cross_value, cross_value),
        whole(sum_cross_output, cross_output),
        small[2],
        small[3],
        whole(sum_expand, expand_weight),
        whole(sum_reduce, reduce_weight),
        small[4],
        small[5],
        whole(sum_vision, vision_proj),
    )


def solution(mesh):
    placed = (
        P(("mod", "dp"), None),
        P(("mod", "dp"), None, None),
        P(("mod", "dp"), None),
        P(("mod", "dp"), None),
        P(("mod", "dp"), None, None),
        P(("mod", "dp"), None),
        P(),
        P(),
        P(),
        P(),
        P(),
        P(),
        P(),
        P(),
        P(),
        P(),
        P(),
        P(),
        P(),
        P(),
        P(),
        P(),
        P(),
    )
    return jax.shard_map(
        on_device,
        mesh=mesh,
        in_specs=placed,
        out_specs=(
            P(("mod", "dp"), None),
            P(("mod", "dp"), None),
            P(("mod", "dp"), None, None),
            P(),
            P(),
            P(),
            P(),
            P(),
            P(),
            P(),
            P(),
            P(),
            P(),
            P(),
            P(),
            P(),
            P(),
            P(),
            P(),
            P(),
        ),
        check_vma=False,
    )
```

```python
import functools

import jax
import jax.numpy as jnp
from jax import lax
from jax.experimental import pallas as pl
from jax.experimental.pallas import tpu as pltpu
from jax.sharding import PartitionSpec as P

HEAD_DIM = 64
TOK_DEV = 768
PATCH_ROWS = 160
FF_TILE = 768
ROW_TILE = 128
OUT_TILE = 768
LONGEST = 40
WINDOW = 64
SLOTS = 128
LANES = 256
BASES = (0, 128, 384, 512)
TOGETHER = 4
TAKES = {
    "self_attend": 8,
    "cross_attend": 9,
    "feed_forward": 17,
    "feed_back": 15,
    "cross_attend_back": 21,
    "self_attend_back": 13,
    "first_back": 5,
    "text_back": 4,
    "patch_back": 5,
    "reduce_terms": 5,
    "expand_terms": 8,
    "cross_terms": 10,
}


def cost(name):
    return pl.CostEstimate(
        flops=TAKES.get(name, 4) * 1_100_000_000, bytes_accessed=1 << 16, transcendentals=0
    )


def norm_rows(values, gain_row, shift_row):
    centred = values - jnp.mean(values, axis=-1, keepdims=True)
    spread = jnp.mean(centred * centred, axis=-1, keepdims=True)
    return centred * lax.rsqrt(spread + 1e-05) * gain_row + shift_row


def matmul(left, right):
    return jnp.dot(left, right, preferred_element_type=jnp.float32)


def norm_rows(values, gain_row, shift_row):
    centred = values - jnp.mean(values, axis=-1, keepdims=True)
    spread = jnp.mean(centred * centred, axis=-1, keepdims=True)
    return centred * lax.rsqrt(spread + 1e-05) * gain_row + shift_row


def matmul(left, right):
    return jnp.dot(left, right, preferred_element_type=jnp.float32)


def slot_of(shape, dim):
    slot = lax.broadcasted_iota(jnp.int32, shape, dim)
    part = (slot >= LONGEST).astype(jnp.int32) + (slot >= 2 * LONGEST).astype(jnp.int32)
    return part, slot - part * LONGEST


def fill_head_masks(masks_ref):
    part, _ = slot_of((SLOTS, LANES), 0)
    lane = lax.broadcasted_iota(jnp.int32, (SLOTS, LANES), 1)
    for odd in range(2):
        low = HEAD_DIM * (part + odd)
        inside = (lane >= low) & (lane < low + HEAD_DIM)
        masks_ref[odd] = jnp.where(inside, 1.0, 0.0).astype(jnp.bfloat16)


def row_place(start):
    first = jnp.minimum(lax.bitwise_and(start, -16), TOK_DEV - WINDOW)
    return pl.multiple_of(first, 16), start - first


def pick_rows(offset, length):
    _, place = slot_of((SLOTS, WINDOW), 0)
    at = lax.broadcasted_iota(jnp.int32, (SLOTS, WINDOW), 1)
    return jnp.where((place < length) & (at == place + offset), 1.0, 0.0).astype(jnp.bfloat16)


def put_rows(offset, length):
    _, place = slot_of((WINDOW, SLOTS), 1)
    at = lax.broadcasted_iota(jnp.int32, (WINDOW, SLOTS), 0)
    return jnp.where((place < length) & (at == place + offset), 1.0, 0.0).astype(jnp.bfloat16)


def dot(left, right, over):
    return lax.dot_general(left, right, (over, ((), ())), preferred_element_type=jnp.float32)


NT = ((1,), (1,))
NN = ((1,), (0,))
TN = ((0,), (0,))


def side_by_side(parts):
    first, second, third, fourth = parts
    half = LANES // 2
    return jnp.concatenate(
        [
            first[:, :half],
            first[:, half:] + second[:, :half],
            second[:, half:],
            third[:, :half],
            third[:, half:] + fourth[:, :half],
            fourth[:, half:],
        ],
        axis=1,
    )


def self_allowed(offset, length):
    at = lax.broadcasted_iota(jnp.int32, (WINDOW, SLOTS), 0)
    return (at >= offset) & (at < offset + length)


def cross_allowed(box_ref, row):
    turn = lax.broadcasted_iota(jnp.int32, (SLOTS, SLOTS), 0)
    chosen = jnp.where(turn == row, 1.0, 0.0).astype(jnp.bfloat16)
    return dot(box_ref[...], chosen, NN) > 0.5


def row_keys(cross, first, image, ref, base):
    if cross:
        return ref[image, :, base : base + LANES]
    return ref[pl.ds(first, WINDOW), base : base + LANES]


def forward_kernel(cross, *refs):
    if cross:
        lengths, images, box_ref, q_ref, k_ref, v_ref, out_ref, log_ref, masks, total = refs
    else:
        lengths, q_ref, k_ref, v_ref, out_ref, log_ref, masks, total = refs
        images = box_ref = None
    fill_head_masks(masks)
    total[...] = jnp.zeros_like(total)

    def rows_at_once(step, start):
        work = []
        for turn in range(TOGETHER):
            row = TOGETHER * step + turn
            length = lengths[0, row]
            first, offset = row_place(start)
            work.append((row, length, images[0, row] if cross else None, first, offset))
            start = start + length
        picked = [
            dot(pick_rows(offset, length), q_ref[pl.ds(first, WINDOW), :], NN)
            for _, length, _, first, offset in work
        ]
        picked = [(p * HEAD_DIM ** (-0.5)).astype(jnp.bfloat16) for p in picked]
        allowed = [
            cross_allowed(box_ref, row) if cross else self_allowed(offset, length)
            for row, length, _, _, offset in work
        ]
        each = [(turn, group) for turn in range(TOGETHER) for group in range(len(BASES))]
        scores = {}
        for turn, group in each:
            _, _, image, first, _ = work[turn]
            base = BASES[group]
            queries = picked[turn][:, base : base + LANES] * masks[group % 2]
            keys_in = row_keys(cross, first, image, k_ref, base)
            scores[turn, group] = dot(keys_in, queries, NT)
        soft = {}
        for turn, group in each:
            row = work[turn][0]
            masked = jnp.where(allowed[turn], scores[turn, group], -1e30)
            top = jnp.max(masked, axis=0, keepdims=True)
            exps = jnp.exp(masked - top)
            summed = jnp.sum(exps, axis=0, keepdims=True)
            soft[turn, group] = (exps * (1.0 / summed)).astype(jnp.bfloat16)
            log_ref[row, group : group + 1, :] = top + jnp.log(summed)
        mixed = {}
        for turn, group in each:
            _, _, image, first, _ = work[turn]
            values_in = row_keys(cross, first, image, v_ref, BASES[group])
            mixed[turn, group] = (
                dot(soft[turn, group], values_in, TN).astype(jnp.bfloat16) * masks[group % 2]
            )
        for turn in range(TOGETHER):
            _, length, _, first, offset = work[turn]
            side = side_by_side([mixed[turn, group] for group in range(len(BASES))])
            total[pl.ds(first, WINDOW), :] += dot(put_rows(offset, length), side, NN)
        return start

    rows = lengths.shape[1]
    lax.fori_loop(0, rows // TOGETHER, rows_at_once, jnp.int32(0))
    out_ref[...] = total[...].astype(out_ref.dtype)


def backward_kernel(cross, *refs):
    if cross:
        lengths, images, box_ref, key_ref, value_ref = refs[:5]
        refs = refs[5:]
        far_ref, refs = refs[8], refs[:8] + refs[9:]
    else:
        lengths, refs = refs[0], refs[1:]
        images = box_ref = None
    q_ref, k_ref, v_ref, g_ref, log_ref, dq_ref, dk_ref, dv_ref, masks, dq, dk, dv = refs
    fill_head_masks(masks)
    dq[...] = jnp.zeros_like(dq)
    dk[...] = jnp.zeros_like(dk)
    dv[...] = jnp.zeros_like(dv)

    def rows_at_once(step, start):
        work = []
        for turn in range(TOGETHER):
            row = TOGETHER * step + turn
            length = lengths[0, row]
            first, offset = row_place(start)
            work.append((row, length, images[0, row] if cross else None, first, offset))
            start = start + length
        picks = [pick_rows(offset, length) for _, length, _, _, offset in work]
        picked = [
            (dot(pick, q_ref[pl.ds(w[3], WINDOW), :], NN) * HEAD_DIM ** (-0.5)).astype(jnp.bfloat16)
            for pick, w in zip(picks, work)
        ]
        picked_g = [
            dot(pick, g_ref[pl.ds(w[3], WINDOW), :], NN).astype(jnp.bfloat16)
            for pick, w in zip(picks, work)
        ]
        allowed = [
            cross_allowed(box_ref, row) if cross else self_allowed(offset, length)
            for row, length, _, _, offset in work
        ]
        each = [(turn, group) for turn in range(TOGETHER) for group in range(len(BASES))]
        queries, grads, scores, grad_soft = {}, {}, {}, {}
        for turn, group in each:
            _, _, image, first, _ = work[turn]
            base = BASES[group]
            mask = masks[group % 2]
            queries[turn, group] = picked[turn][:, base : base + LANES] * mask
            grads[turn, group] = picked_g[turn][:, base : base + LANES] * mask
            keys_in = row_keys(cross, first, image, k_ref, base)
            values_in = row_keys(cross, first, image, v_ref, base)
            scores[turn, group] = dot(keys_in, queries[turn, group], NT)
            grad_soft[turn, group] = dot(values_in, grads[turn, group], NT)
        soft, grad_scores = {}, {}
        for turn, group in each:
            row = work[turn][0]
            masked = jnp.where(allowed[turn], scores[turn, group], -1e30)
            kept = jnp.exp(masked - log_ref[row, group : group + 1, :])
            inner = jnp.sum(kept * grad_soft[turn, group], axis=0, keepdims=True)
            grad_scores[turn, group] = (kept * (grad_soft[turn, group] - inner)).astype(
                jnp.bfloat16
            )
            soft[turn, group] = kept.astype(jnp.bfloat16)
        grad_k, grad_v, grad_q = {}, {}, {}
        for turn, group in each:
            _, _, image, first, _ = work[turn]
            keys_in = row_keys(cross, first, image, k_ref, BASES[group])
            grad_k[turn, group] = dot(grad_scores[turn, group], queries[turn, group], NN)
            grad_v[turn, group] = dot(soft[turn, group], grads[turn, group], NN)
            grad_q[turn, group] = (
                dot(grad_scores[turn, group], keys_in, TN) * HEAD_DIM ** (-0.5)
            ).astype(jnp.bfloat16) * masks[group % 2]
        for turn in range(TOGETHER):
            _, length, image, first, offset = work[turn]
            every = range(len(BASES))
            side_k = side_by_side([grad_k[turn, group] for group in every])
            side_v = side_by_side([grad_v[turn, group] for group in every])
            side_q = side_by_side([grad_q[turn, group] for group in every])
            if cross:
                dk[image] += side_k
                dv[image] += side_v
            else:
                dk[pl.ds(first, WINDOW), :] += side_k
                dv[pl.ds(first, WINDOW), :] += side_v
            dq[pl.ds(first, WINDOW), :] += dot(put_rows(offset, length), side_q, NN)
        return start

    rows = lengths.shape[1]
    lax.fori_loop(0, rows // TOGETHER, rows_at_once, jnp.int32(0))
    dq_ref[...] = dq[...].astype(dq_ref.dtype)
    dk_ref[...] = dk[...].astype(dk_ref.dtype)
    dv_ref[...] = dv[...].astype(dv_ref.dtype)
    if cross:

        def project(image, _):
            projected = dot(dk_ref[image], key_ref[...], NT) + dot(dv_ref[image], value_ref[...], NT)
            far_ref[image] = projected.astype(far_ref.dtype)
            return _

        lax.fori_loop(0, k_ref.shape[0], project, 0)


def in_smem():
    return pl.BlockSpec(memory_space=pltpu.SMEM)


def in_vmem():
    return pl.BlockSpec(memory_space=pltpu.VMEM)


def attend(scalars, queries, keys_in, values_in, box):
    cross = box is not None
    rows = scalars[0].shape[1]
    tensors = ((box,) if cross else ()) + (queries, keys_in, values_in)
    return pl.pallas_call(
        functools.partial(forward_kernel, cross),
        out_shape=(
            jax.ShapeDtypeStruct(queries.shape, jnp.bfloat16),
            jax.ShapeDtypeStruct((rows, len(BASES), SLOTS), jnp.float32),
        ),
        in_specs=[in_smem()] * len(scalars) + [in_vmem()] * len(tensors),
        out_specs=(in_vmem(), in_vmem()),
        scratch_shapes=[
            pltpu.VMEM((2, SLOTS, LANES), jnp.bfloat16),
            pltpu.VMEM(queries.shape, jnp.float32),
        ],
        compiler_params=pltpu.CompilerParams(vmem_limit_bytes=24 << 20),
        cost_estimate=cost("cross_attend" if cross else "self_attend"),
        name="cross_attend" if cross else "self_attend",
    )(*scalars, *tensors)


def attend_back(scalars, queries, keys_in, values_in, grads, logs, extra=()):
    cross = bool(extra)
    tensors = extra + (queries, keys_in, values_in, grads, logs)
    results = (queries, keys_in, values_in) + ((keys_in,) if cross else ())
    return pl.pallas_call(
        functools.partial(backward_kernel, cross),
        out_shape=tuple(jax.ShapeDtypeStruct(a.shape, jnp.bfloat16) for a in results),
        in_specs=[in_smem()] * len(scalars) + [in_vmem()] * len(tensors),
        out_specs=(in_vmem(),) * len(results),
        scratch_shapes=[
            pltpu.VMEM((2, SLOTS, LANES), jnp.bfloat16),
            pltpu.VMEM(queries.shape, jnp.float32),
            pltpu.VMEM(keys_in.shape, jnp.float32),
            pltpu.VMEM(keys_in.shape, jnp.float32),
        ],
        compiler_params=pltpu.CompilerParams(vmem_limit_bytes=28 << 20),
        cost_estimate=cost("cross_attend_back" if cross else "self_attend_back"),
        name="cross_attend_back" if cross else "self_attend_back",
    )(*scalars, *tensors)


def phi_parts(values):
    size = jnp.abs(values)
    tail = jnp.exp(-0.5 * values * values)
    turn = 1.0 / (1.0 + (0.3275911 * 0.5**0.5) * size)
    series = 1.061405429 * turn - 1.453152027
    series = series * turn + 1.421413741
    series = series * turn - 0.284496736
    series = series * turn + 0.254829592
    half = (0.5 * turn) * series * tail
    return jnp.where(values >= 0, 1.0 - half, half), tail * 0.3989422804014327


def centre(values):
    off = values - jnp.mean(values, axis=-1, keepdims=True)
    scale = lax.rsqrt(jnp.mean(off * off, axis=-1, keepdims=True) + 1e-05)
    return off * scale, scale


def centre_back(grads, normed, scale, gain):
    inner = grads * gain
    mean = jnp.mean(inner, axis=-1, keepdims=True)
    along = jnp.mean(inner * normed, axis=-1, keepdims=True)
    return scale * (inner - mean - normed * along)


def total_rows(values):
    return jnp.sum(values, axis=0, keepdims=True)


def feed_forward_kernel(
    x_ref, xb_ref, expand_ref, reduce_ref, cot_ref, gain_ref, shift_ref,
    active_ref, slope_ref, merged_ref, third_ref, third_b_ref, dgain_ref, dshift_ref, held, acc,
):
    tokens, width = x_ref.shape
    inner = expand_ref.shape[1]
    tiles = inner // FF_TILE

    def hide(tile, slot):
        lanes = pl.ds(pl.multiple_of(tile * FF_TILE, FF_TILE), FF_TILE)
        held[slot] = dot(xb_ref[...], expand_ref[:, lanes], NN)

    def activate(tile, slot):
        lanes = pl.ds(pl.multiple_of(tile * FF_TILE, FF_TILE), FF_TILE)
        hidden = held[slot]
        share, density = phi_parts(hidden)
        active_ref[:, lanes] = (hidden * share).astype(jnp.bfloat16)
        slope_ref[:, lanes] = (share + hidden * density).astype(jnp.bfloat16)

    hide(0, 0)

    def both(pair, _):
        for slot in range(2):
            tile = 2 * pair + slot
            hide(tile + 1, 1 - slot)
            activate(tile, slot)
        return _

    lax.fori_loop(0, tiles // 2 - 1, both, 0)
    hide(tiles - 1, 1)
    activate(tiles - 2, 0)
    activate(tiles - 1, 1)

    def project(tile, _):
        lanes = pl.ds(pl.multiple_of(tile * OUT_TILE, OUT_TILE), OUT_TILE)
        acc[:, lanes] = x_ref[:, lanes] + dot(active_ref[...], reduce_ref[:, lanes], NN)
        return _

    lax.fori_loop(0, width // OUT_TILE, project, 0)
    dgain_ref[...] = jnp.zeros_like(dgain_ref)
    dshift_ref[...] = jnp.zeros_like(dshift_ref)

    def finish(part, _):
        rows = pl.ds(pl.multiple_of(part * ROW_TILE, ROW_TILE), ROW_TILE)
        normed, scale = centre(acc[rows, :])
        merged_ref[rows, :] = (normed * gain_ref[...] + shift_ref[...]).astype(jnp.bfloat16)
        grads = cot_ref[rows, :].astype(jnp.float32)
        third = centre_back(grads, normed, scale, gain_ref[...])
        third_ref[rows, :] = third
        third_b_ref[rows, :] = third.astype(jnp.bfloat16)
        dgain_ref[...] += total_rows(grads * normed)
        dshift_ref[...] += total_rows(grads)
        return _

    lax.fori_loop(0, tokens // ROW_TILE, finish, 0)


def feed_forward(x, xb, expand, reduce, cot, gain, shift):
    tokens, width = x.shape
    inner = expand.shape[1]
    wide = lambda dtype: jax.ShapeDtypeStruct((tokens, inner), dtype)
    square = lambda dtype: jax.ShapeDtypeStruct((tokens, width), dtype)
    flat = jax.ShapeDtypeStruct((1, width), jnp.float32)
    return pl.pallas_call(
        feed_forward_kernel,
        in_specs=[in_vmem()] * 7,
        out_specs=(in_vmem(),) * 7,
        out_shape=(
            wide(jnp.bfloat16), wide(jnp.bfloat16), square(jnp.bfloat16),
            square(jnp.float32), square(jnp.bfloat16), flat, flat,
        ),
        scratch_shapes=[
            pltpu.VMEM((2, tokens, FF_TILE), jnp.float32), pltpu.VMEM((tokens, width), jnp.float32)
        ],
        compiler_params=pltpu.CompilerParams(vmem_limit_bytes=24 << 20),
        cost_estimate=cost("feed_forward"),
        name="feed_forward",
    )(x, xb, expand, reduce, cot, gain[None], shift[None])


def feed_back_kernel(
    third_ref, third_b_ref, slope_ref, expand_ref, reduce_ref, second_ref, gain_ref, cross_out_ref,
    hidden_ref, grad_ref, grad_b_ref, crossed_ref, dgain_ref, dshift_ref, acc,
):
    step = pl.program_id(0)
    active = dot(third_b_ref[...], reduce_ref[...], NT)
    hidden = (active * slope_ref[...].astype(jnp.float32)).astype(jnp.bfloat16)
    hidden_ref[...] = hidden
    part = dot(hidden, expand_ref[...], NT)

    @pl.when(step == 0)
    def _():
        acc[...] = third_ref[...] + part

    @pl.when(step > 0)
    def _():
        acc[...] += part

    @pl.when(step == pl.num_programs(0) - 1)
    def _():
        norm_back(acc, second_ref, gain_ref, grad_ref, grad_b_ref, dgain_ref, dshift_ref)
        crossed_ref[...] = dot(grad_b_ref[...], cross_out_ref[...], NT).astype(jnp.bfloat16)


def norm_back(upstream, summed_ref, gain_ref, grad_ref, grad_b_ref, dgain_ref, dshift_ref):
    dgain_ref[...] = jnp.zeros_like(dgain_ref)
    dshift_ref[...] = jnp.zeros_like(dshift_ref)

    def some_rows(part, _):
        rows = pl.ds(pl.multiple_of(part * ROW_TILE, ROW_TILE), ROW_TILE)
        normed, scale = centre(summed_ref[rows, :])
        grads = upstream[rows, :]
        grad = centre_back(grads, normed, scale, gain_ref[...])
        grad_ref[rows, :] = grad
        grad_b_ref[rows, :] = grad.astype(jnp.bfloat16)
        dgain_ref[...] += total_rows(grads * normed)
        dshift_ref[...] += total_rows(grads)
        return _

    lax.fori_loop(0, summed_ref.shape[0] // ROW_TILE, some_rows, 0)


def feed_back(third, third_b, slope, expand, reduce, second_sum, gain, cross_out):
    tokens, width = third.shape
    inner = expand.shape[1]
    square = lambda dtype: jax.ShapeDtypeStruct((tokens, width), dtype)
    flat = jax.ShapeDtypeStruct((1, width), jnp.float32)
    tile = pl.BlockSpec((tokens, FF_TILE), lambda i: (0, i))
    return pl.pallas_call(
        feed_back_kernel,
        grid=(inner // FF_TILE,),
        in_specs=[
            in_vmem(),
            in_vmem(),
            tile,
            pl.BlockSpec((width, FF_TILE), lambda i: (0, i)),
            pl.BlockSpec((FF_TILE, width), lambda i: (i, 0)),
            in_vmem(),
            in_vmem(),
            in_vmem(),
        ],
        out_specs=(tile,) + (in_vmem(),) * 5,
        out_shape=(
            jax.ShapeDtypeStruct((tokens, inner), jnp.bfloat16), square(jnp.float32),
            square(jnp.bfloat16), square(jnp.bfloat16), flat, flat,
        ),
        scratch_shapes=[pltpu.VMEM((tokens, width), jnp.float32)],
        compiler_params=pltpu.CompilerParams(vmem_limit_bytes=36 << 20),
        cost_estimate=cost("feed_back"),
        name="feed_back",
    )(third, third_b, slope, expand, reduce, second_sum, gain[None], cross_out)


def first_back_kernel(
    gq_ref, query_ref, second_ref, first_ref, gain_ref, output_ref,
    grad_ref, grad_b_ref, attended_ref, dgain_ref, dshift_ref, acc,
):
    acc[...] = second_ref[...] + dot(gq_ref[...], query_ref[...], NT)
    norm_back(acc, first_ref, gain_ref, grad_ref, grad_b_ref, dgain_ref, dshift_ref)
    attended_ref[...] = dot(grad_b_ref[...], output_ref[...], NT).astype(jnp.bfloat16)


def first_back(grad_query, cross_query, grad_second, first_sum, gain, self_output):
    square = lambda dtype: jax.ShapeDtypeStruct(first_sum.shape, dtype)
    flat = jax.ShapeDtypeStruct((1, first_sum.shape[1]), jnp.float32)
    return plain_call(
        first_back_kernel,
        (square(jnp.float32), square(jnp.bfloat16), square(jnp.bfloat16), flat, flat),
        (grad_query, cross_query, grad_second, first_sum, gain[None], self_output),
        [pltpu.VMEM(first_sum.shape, jnp.float32)],
        "first_back",
    )


def plain_call(kernel, out_shape, arrays, scratch, name, scalars=()):
    return pl.pallas_call(
        kernel,
        out_shape=out_shape,
        in_specs=[in_smem()] * len(scalars) + [in_vmem()] * len(arrays),
        out_specs=jax.tree.map(lambda _: in_vmem(), out_shape),
        scratch_shapes=scratch,
        compiler_params=pltpu.CompilerParams(vmem_limit_bytes=24 << 20),
        cost_estimate=cost(name),
        name=name,
    )(*scalars, *arrays)


def text_back_kernel(first_ref, *refs):
    out_ref = refs[-1]
    out_ref[...] = first_ref[...]
    for grad_ref, weight_ref in zip(refs[:3], refs[3:6]):
        out_ref[...] += dot(grad_ref[...], weight_ref[...], NT)


def text_back(grad_first, grads, weights):
    shape = jax.ShapeDtypeStruct(grad_first.shape, jnp.float32)
    return plain_call(text_back_kernel, shape, (grad_first, *grads, *weights), [], "text_back")


def patch_back_kernel(grad_ref, weight_ref, out_ref):
    for image in range(out_ref.shape[0]):
        rows = grad_ref[image * PATCH_ROWS : (image + 1) * PATCH_ROWS]
        out_ref[image] = dot(rows, weight_ref[...], NT)[: out_ref.shape[1]]


def patch_back(grad_projected, vision_proj, shape):
    return plain_call(
        patch_back_kernel,
        jax.ShapeDtypeStruct(shape, jnp.float32),
        (grad_projected, vision_proj),
        [],
        "patch_back",
    )


def terms_of(pieces, arrays, shape, name, turned=None):
    def kernel(core_ref, *refs):
        keep, away = refs[len(arrays) : len(arrays) + 2]
        scratch = refs[len(arrays) + 2 :]

        def put(half, shards, rows, columns, product):
            values = product.astype(jnp.bfloat16)
            values = values.reshape((-1, values.shape[0] // 16 if shards is None else shards[1], values.shape[1]))
            first = slice(None) if shards is None else shards[0]

            def store(ref):
                ref[first, rows, columns] = values

            pl.when(core_ref[0] == half)(lambda: store(keep))
            pl.when(core_ref[0] != half)(lambda: store(away))

        pieces(refs[: len(arrays)], scratch, put)

    out = jax.ShapeDtypeStruct(shape, jnp.bfloat16)
    scratch = [] if turned is None else [pltpu.VMEM(turned, jnp.bfloat16)]
    return plain_call(kernel, (out, out), arrays, scratch, name, (my_bit(*CORE)[None],))


def reduce_terms(refs, scratch, put):
    active, grads = refs
    blocks = active.shape[1] // FF_TILE
    rows = active.shape[1] // 16
    held = 16 // blocks

    def block(at, _):
        lanes = pl.ds(pl.multiple_of(at * FF_TILE, FF_TILE), FF_TILE)
        product = dot(active[:, lanes], grads[...], TN)
        half = product.shape[1] // 2
        shards = (pl.ds(at * held, held), rows)
        put(0, shards, slice(None), slice(None), product[:, :half])
        put(1, shards, slice(None), slice(None), product[:, half:])
        return _

    lax.fori_loop(0, blocks, block, 0)


def expand_terms(refs, scratch, put):
    values, grads = refs
    (turned,) = scratch
    turned[...] = values[...].T
    blocks = grads.shape[1] // FF_TILE

    for at in range(blocks):
        product = dot(turned[...], grads[:, at * FF_TILE : (at + 1) * FF_TILE], NN)
        place = at % (blocks // 2)
        columns = slice(place * FF_TILE, (place + 1) * FF_TILE)
        put(at // (blocks // 2), None, slice(None), columns, product)


def cross_terms(refs, scratch, put):
    crossed, grad_second, normed_one, grad_query, far, grad_key, grad_value = refs
    width = crossed.shape[1]
    left, right = slice(0, width), slice(width, 2 * width)
    put(0, None, slice(None), left, dot(crossed[...], grad_second[...], TN))
    put(0, None, slice(None), right, dot(normed_one[...], grad_query[...], TN))
    put(1, None, slice(None), left, dot(far[...], grad_key[...], TN))
    put(1, None, slice(None), right, dot(far[...], grad_value[...], TN))


def pair_terms(refs, scratch, put):
    left, left_grad, right, right_grad = refs
    every = slice(None)
    put(0, None, every, every, dot(left[...], left_grad[...], TN))
    put(1, None, every, every, dot(right[...], right_grad[...], TN))


def vision_terms(refs, scratch, put):
    patches, grads = refs
    half = patches.shape[1] // 2
    every = slice(None)
    put(0, None, every, every, dot(patches[:, :half], grads[...], TN))
    put(1, None, every, every, dot(patches[:, half:], grads[...], TN))


def box_columns(box_mask, patch_rows):
    turned = jnp.transpose(box_mask).astype(jnp.bfloat16)
    return jnp.pad(
        turned, ((0, patch_rows - turned.shape[0]), (0, SLOTS - turned.shape[1]))
    )


def flip_bit(values, axis, bit):
    count = lax.axis_size(axis)
    return lax.ppermute(values, axis, [(i, i ^ (1 << bit)) for i in range(count)])


def my_bit(axis, bit):
    return (lax.axis_index(axis) >> bit) & 1


def stage_order(names):
    bits = {"x": [("dp", 1)], "y": [("mod", 0)], "z": [("dp", 2), ("dp", 3)]}
    return sum([bits[name] for name in names], [])


def other_bits():
    dp_bits = lax.axis_size("dp").bit_length() - 1
    mod_bits = lax.axis_size("mod").bit_length() - 1
    return [("mod", bit) for bit in range(1, mod_bits)] + [("dp", bit) for bit in range(4, dp_bits)]


CORE = ("dp", 0)
ORDERS = {"r": "yxz", "e": "zxy", "c": "xyz", "s": "yxz", "q": "yxz", "v": "xyz"}
TURNS = "PergAvcrTvscvgerqvcesvrcgvesqvcesvrcseqgvsVqsqcsrqeqsRSqceCEqQ"


def place_in(order):
    place = jnp.int32(0)
    for axis, bit in order:
        place = 2 * place + my_bit(axis, bit)
    return place


class Sum:
    def __init__(self, keep, away, order):
        self.order = order = stage_order(order)
        self.kept = keep
        self.flown = flip_bit(away, *CORE)
        self.steps = [("scatter", stage) for stage in order]
        self.steps += [("add", stage) for stage in other_bits()]
        self.steps += [("gather", stage) for stage in reversed(order)] + [("last", CORE)]
        self.before = "add"

    def advance(self):
        if self.before == "add":
            values = self.kept + self.flown
        else:
            values = jnp.concatenate([self.kept, self.flown], axis=0)
        kind, (axis, bit) = self.steps.pop(0)
        if kind == "scatter":
            mine = my_bit(axis, bit)
            pair = values.reshape((2, values.shape[0] // 2) + values.shape[1:])
            away = lax.dynamic_index_in_dim(pair, 1 - mine, 0, False)
            self.kept = lax.dynamic_index_in_dim(pair, mine, 0, False)
        else:
            self.kept = away = values
        self.flown = flip_bit(away, axis, bit)
        self.before = "add" if kind in ("scatter", "add") else "gather"


class Line:
    def __init__(self):
        self.token = jnp.zeros((1, 1), jnp.float32)

    def meet(self, values, *sums):
        flown = [one.flown for one in sums]
        values, self.token, flown = lax.optimization_barrier((values, self.token, flown))
        for one, arrived in zip(sums, flown):
            one.flown = arrived
            if one.steps:
                one.advance()
        return values


class SmallSum:
    def __init__(self, values):
        self.steps = [CORE] + stage_order("xyz") + other_bits()
        self.kept = values
        self.flown = jnp.zeros_like(values)
        self.advance()

    def advance(self):
        self.kept = self.kept + self.flown
        self.flown = flip_bit(self.kept, *self.steps.pop(0))

    @property
    def total(self):
        return self.kept + self.flown


def spread(one, shapes, fill, name):
    own, other = one.kept, one.flown
    shards, rows, columns = own.shape
    at = jnp.stack([my_bit(*CORE), place_in(one.order)])

    def kernel(at_ref, own_ref, other_ref, *outs):
        inner = at_ref[1] & 3

        def write(low, high):
            for step in range(4):
                fill(low.at[step ^ inner], high.at[step ^ inner], outs, step)

        pl.when(at_ref[0] == 0)(lambda: write(own_ref, other_ref))
        pl.when(at_ref[0] == 1)(lambda: write(other_ref, own_ref))

    def block_of(shape):
        lead = len(shape) - 3
        return pl.BlockSpec(
            shape[:lead] + (4,) + shape[lead + 1 :],
            lambda i, at_ref: (0,) * lead + (i, 0, 0),
        )

    taken = pl.BlockSpec((4, rows, columns), lambda i, at_ref: (i ^ (at_ref[1] >> 2), 0, 0))
    return pl.pallas_call(
        kernel,
        out_shape=tuple(jax.ShapeDtypeStruct(shape, jnp.float32) for shape in shapes),
        grid_spec=pltpu.PrefetchScalarGridSpec(
            num_scalar_prefetch=1,
            grid=(shards // 4,),
            in_specs=[taken, taken],
            out_specs=tuple(block_of(shape) for shape in shapes),
        ),
        compiler_params=pltpu.CompilerParams(vmem_limit_bytes=24 << 20),
        cost_estimate=pl.CostEstimate(
            flops=0, bytes_accessed=12 * own.size, transcendentals=0
        ),
        name=name,
    )(at, own, other)


def fill_columns(low, high, outs, step):
    columns = low.shape[-1]
    outs[0][step, :, :columns] = low[...].astype(jnp.float32)
    outs[0][step, :, columns:] = high[...].astype(jnp.float32)


def fill_couples(low, high, outs, step):
    columns = low.shape[-1] // 2
    for half, taken in enumerate((low, high)):
        outs[2 * half][step] = taken[:, :columns].astype(jnp.float32)
        outs[2 * half + 1][step] = taken[:, columns:].astype(jnp.float32)


def fill_each(low, high, outs, step):
    outs[0][step] = low[...].astype(jnp.float32)
    outs[1][step] = high[...].astype(jnp.float32)


def fill_halves(low, high, outs, step):
    outs[0][0, step] = low[...].astype(jnp.float32)
    outs[0][1, step] = high[...].astype(jnp.float32)


def on_device(
    text_tokens,
    patches,
    lengths,
    row_image,
    box_mask,
    cotangent,
    self_query,
    self_key,
    self_value,
    self_output,
    first_gain,
    first_bias,
    cross_query,
    cross_key,
    cross_value,
    cross_output,
    second_gain,
    second_bias,
    expand_weight,
    reduce_weight,
    third_gain,
    third_bias,
    vision_proj,
):
    image_count = patches.shape[0]
    box = box_columns(box_mask[0], PATCH_ROWS)
    patch_count = patches.shape[1]
    flat_patches = jnp.pad(patches, ((0, 0), (0, PATCH_ROWS - patch_count), (0, 0))).reshape(
        image_count * PATCH_ROWS, patches.shape[2]
    )

    def by_image(values):
        return values.reshape(image_count, PATCH_ROWS, values.shape[-1])

    projected = matmul(flat_patches, vision_proj).astype(jnp.bfloat16)
    far_projected = flip_bit(projected, "mod", 0)
    query_s = matmul(text_tokens, self_query).astype(jnp.bfloat16)
    key_s = matmul(text_tokens, self_key).astype(jnp.bfloat16)
    value_s = matmul(text_tokens, self_value).astype(jnp.bfloat16)
    attended_b, self_log = attend((lengths,), query_s, key_s, value_s, None)
    first_sum = text_tokens.astype(jnp.float32) + matmul(attended_b, self_output)
    normed_one = norm_rows(first_sum, first_gain, first_bias)
    normed_one_b = normed_one.astype(jnp.bfloat16)
    query_c = matmul(normed_one_b, cross_query).astype(jnp.bfloat16)
    far_keys = by_image(matmul(far_projected, cross_key).astype(jnp.bfloat16))
    far_values = by_image(matmul(far_projected, cross_value).astype(jnp.bfloat16))
    crossed_b, cross_log = attend((lengths, row_image), query_c, far_keys, far_values, box)
    second_sum = normed_one + matmul(crossed_b, cross_output)
    normed_two = norm_rows(second_sum, second_gain, second_bias)
    normed_two_b = normed_two.astype(jnp.bfloat16)
    activated_b, slope, merged, grad_third, grad_third_b, grad_third_gain, grad_third_bias = (
        feed_forward(
            normed_two, normed_two_b, expand_weight, reduce_weight, cotangent, third_gain, third_bias
        )
    )
    line = Line()
    width = text_tokens.shape[1]
    inner = expand_weight.shape[1]
    sums = {}
    sums["r"] = Sum(
        *terms_of(
            reduce_terms, (activated_b, grad_third_b), (16, inner // 16, width // 2), "reduce_terms"
        ),
        ORDERS["r"],
    )
    (
        grad_hidden,
        grad_second,
        grad_second_b,
        grad_crossed,
        grad_second_gain,
        grad_second_bias,
    ) = feed_back(
        grad_third,
        grad_third_b,
        slope,
        expand_weight,
        reduce_weight,
        second_sum,
        second_gain,
        cross_output,
    )
    grad_hidden, grad_crossed = line.meet((grad_hidden, grad_crossed), sums["r"])
    sums["e"] = Sum(
        *terms_of(
            expand_terms,
            (normed_two_b, grad_hidden),
            (16, width // 16, inner // 2),
            "expand_terms",
            normed_two_b.shape,
        ),
        ORDERS["e"],
    )
    grad_crossed, sums["e"].kept = line.meet((grad_crossed, sums["e"].kept))
    grads_cross = attend_back(
        (lengths, row_image),
        query_c,
        far_keys,
        far_values,
        grad_crossed,
        cross_log,
        (box, cross_key, cross_value),
    )
    grads_cross = line.meet(grads_cross, sums["e"], sums["r"])
    grad_query_c, grad_far_keys, grad_far_values, grad_far_projected = grads_cross
    grad_far_keys = grad_far_keys.reshape(projected.shape)
    grad_far_values = grad_far_values.reshape(projected.shape)
    grad_projected = flip_bit(grad_far_projected.reshape(projected.shape), "mod", 0)
    grad_first, grad_first_b, grad_attended, grad_first_gain, grad_first_bias = first_back(
        grad_query_c, cross_query, grad_second, first_sum, first_gain, self_output
    )
    small_sum = SmallSum(
        jnp.concatenate(
            [
                grad_first_gain,
                grad_first_bias,
                grad_second_gain,
                grad_second_bias,
                grad_third_gain,
                grad_third_bias,
            ]
        )
    )
    sums["g"] = small_sum
    grad_attended, grad_far_values = line.meet((grad_attended, grad_far_values))
    sums["c"] = Sum(
        *terms_of(
            cross_terms,
            (
                crossed_b,
                grad_second_b,
                normed_one_b,
                grad_query_c,
                far_projected,
                grad_far_keys,
                grad_far_values,
            ),
            (16, width // 16, 2 * width),
            "cross_terms",
        ),
        ORDERS["c"],
    )
    grad_attended = line.meet(grad_attended, sums["r"])
    grad_attended = line.meet(grad_attended, sums["c"], sums["g"])
    patch_grad = patch_back(grad_projected, vision_proj, patches.shape)
    half = vision_proj.shape[0] // 2
    tall = (16, half // 16, width)
    sums["v"] = Sum(
        *terms_of(vision_terms, (flat_patches, grad_projected), tall, "vision_terms"), ORDERS["v"]
    )
    square = (16, width // 16, width)

    def pair_sum(name, order, *arrays):
        return Sum(*terms_of(pair_terms, arrays, square, name), order)

    spreads = {}
    for turn in TURNS:
        if turn == "A":
            grad_attended = line.meet(grad_attended)
            grads_self = attend_back((lengths,), query_s, key_s, value_s, grad_attended, self_log)
            grads_self = line.meet(grads_self)
            grad_query_s, grad_key_s, grad_value_s = grads_self
            sums["s"] = pair_sum(
                "self_terms_one", ORDERS["s"], attended_b, grad_first_b, text_tokens, grad_key_s
            )
            sums["q"] = pair_sum(
                "self_terms_two", ORDERS["q"], text_tokens, grad_query_s, text_tokens, grad_value_s
            )
            text_grad = text_back(grad_first, grads_self, (self_query, self_key, self_value))
        elif turn == "T":
            text_grad = line.meet(text_grad)
        elif turn == "P":
            patch_grad = line.meet(patch_grad)
        elif turn.isupper():
            one = sums[turn.lower()]
            while one.steps:
                line.meet((), one)
            line.meet((), one)
            shapes, fill = {
                "R": ([(16,) + (inner // 16, width)], fill_columns),
                "E": ([(16,) + (width // 16, inner)], fill_columns),
                "C": ([square] * 4, fill_couples),
                "S": ([square] * 2, fill_each),
                "Q": ([square] * 2, fill_each),
                "V": ([(2,) + tall], fill_halves),
            }[turn]
            spreads[turn] = line.meet(spread(one, shapes, fill, "spread_" + turn.lower()))
        else:
            line.meet((), sums[turn])
    while small_sum.steps:
        line.meet((), small_sum)
    small = line.meet(small_sum.total) + line.token
    (sum_reduce,) = spreads["R"]
    (sum_expand,) = spreads["E"]
    sum_cross_output, sum_cross_query, sum_cross_key, sum_cross_value = spreads["C"]
    sum_self_output, sum_self_key = spreads["S"]
    sum_self_query, sum_self_value = spreads["Q"]
    (sum_vision,) = spreads["V"]

    def whole(values, like):
        return values.reshape(like.shape)

    return (
        merged,
        text_grad,
        patch_grad,
        whole(sum_self_query, self_query),
        whole(sum_self_key, self_key),
        whole(sum_self_value, self_value),
        whole(sum_self_output, self_output),
        small[0],
        small[1],
        whole(sum_cross_query, cross_query),
        whole(sum_cross_key, cross_key),
        whole(sum_cross_value, cross_value),
        whole(sum_cross_output, cross_output),
        small[2],
        small[3],
        whole(sum_expand, expand_weight),
        whole(sum_reduce, reduce_weight),
        small[4],
        small[5],
        whole(sum_vision, vision_proj),
    )


def solution(mesh):
    placed = (
        P(("mod", "dp"), None),
        P(("mod", "dp"), None, None),
        P(("mod", "dp"), None),
        P(("mod", "dp"), None),
        P(("mod", "dp"), None, None),
        P(("mod", "dp"), None),
        P(),
        P(),
        P(),
        P(),
        P(),
        P(),
        P(),
        P(),
        P(),
        P(),
        P(),
        P(),
        P(),
        P(),
        P(),
        P(),
        P(),
    )
    return jax.shard_map(
        on_device,
        mesh=mesh,
        in_specs=placed,
        out_specs=(
            P(("mod", "dp"), None),
            P(("mod", "dp"), None),
            P(("mod", "dp"), None, None),
            P(),
            P(),
            P(),
            P(),
            P(),
            P(),
            P(),
            P(),
            P(),
            P(),
            P(),
            P(),
            P(),
            P(),
            P(),
            P(),
            P(),
        ),
        check_vma=False,
    )
```

```python
import functools

import jax
import jax.numpy as jnp
from jax import lax
from jax.experimental import pallas as pl
from jax.experimental.pallas import tpu as pltpu
from jax.sharding import PartitionSpec as P

HEAD_DIM = 64
TOK_DEV = 768
PATCH_ROWS = 160
FF_TILE = 768
ROW_TILE = 128
OUT_TILE = 768
LONGEST = 40
WINDOW = 64
SLOTS = 128
LANES = 256
BASES = (0, 128, 384, 512)
TOGETHER = 4
TAKES = {
    "self_attend": 8,
    "cross_attend": 9,
    "feed_forward": 17,
    "feed_back": 15,
    "cross_attend_back": 21,
    "self_attend_back": 13,
    "first_back": 5,
    "text_back": 4,
    "patch_back": 5,
    "reduce_terms": 5,
    "expand_terms": 8,
    "cross_terms": 10,
}


def cost(name):
    return pl.CostEstimate(
        flops=TAKES.get(name, 4) * 1_100_000_000, bytes_accessed=1 << 16, transcendentals=0
    )


def norm_rows(values, gain_row, shift_row):
    centred = values - jnp.mean(values, axis=-1, keepdims=True)
    spread = jnp.mean(centred * centred, axis=-1, keepdims=True)
    return centred * lax.rsqrt(spread + 1e-05) * gain_row + shift_row


def matmul(left, right):
    return jnp.dot(left, right, preferred_element_type=jnp.float32)


def norm_rows(values, gain_row, shift_row):
    centred = values - jnp.mean(values, axis=-1, keepdims=True)
    spread = jnp.mean(centred * centred, axis=-1, keepdims=True)
    return centred * lax.rsqrt(spread + 1e-05) * gain_row + shift_row


def matmul(left, right):
    return jnp.dot(left, right, preferred_element_type=jnp.float32)


def slot_of(shape, dim):
    slot = lax.broadcasted_iota(jnp.int32, shape, dim)
    part = (slot >= LONGEST).astype(jnp.int32) + (slot >= 2 * LONGEST).astype(jnp.int32)
    return part, slot - part * LONGEST


def fill_head_masks(masks_ref):
    part, _ = slot_of((SLOTS, LANES), 0)
    lane = lax.broadcasted_iota(jnp.int32, (SLOTS, LANES), 1)
    for odd in range(2):
        low = HEAD_DIM * (part + odd)
        inside = (lane >= low) & (lane < low + HEAD_DIM)
        masks_ref[odd] = jnp.where(inside, 1.0, 0.0).astype(jnp.bfloat16)


def row_place(start):
    first = jnp.minimum(lax.bitwise_and(start, -16), TOK_DEV - WINDOW)
    return pl.multiple_of(first, 16), start - first


def pick_rows(offset, length):
    _, place = slot_of((SLOTS, WINDOW), 0)
    at = lax.broadcasted_iota(jnp.int32, (SLOTS, WINDOW), 1)
    return jnp.where((place < length) & (at == place + offset), 1.0, 0.0).astype(jnp.bfloat16)


def put_rows(offset, length):
    _, place = slot_of((WINDOW, SLOTS), 1)
    at = lax.broadcasted_iota(jnp.int32, (WINDOW, SLOTS), 0)
    return jnp.where((place < length) & (at == place + offset), 1.0, 0.0).astype(jnp.bfloat16)


def dot(left, right, over):
    return lax.dot_general(left, right, (over, ((), ())), preferred_element_type=jnp.float32)


NT = ((1,), (1,))
NN = ((1,), (0,))
TN = ((0,), (0,))


def side_by_side(parts):
    first, second, third, fourth = parts
    half = LANES // 2
    return jnp.concatenate(
        [
            first[:, :half],
            first[:, half:] + second[:, :half],
            second[:, half:],
            third[:, :half],
            third[:, half:] + fourth[:, :half],
            fourth[:, half:],
        ],
        axis=1,
    )


def self_allowed(offset, length):
    at = lax.broadcasted_iota(jnp.int32, (WINDOW, SLOTS), 0)
    return (at >= offset) & (at < offset + length)


def cross_allowed(box_ref, row):
    turn = lax.broadcasted_iota(jnp.int32, (SLOTS, SLOTS), 0)
    chosen = jnp.where(turn == row, 1.0, 0.0).astype(jnp.bfloat16)
    return dot(box_ref[...], chosen, NN) > 0.5


def row_keys(cross, first, image, ref, base):
    if cross:
        return ref[image, :, base : base + LANES]
    return ref[pl.ds(first, WINDOW), base : base + LANES]


def forward_kernel(cross, *refs):
    if cross:
        lengths, images, box_ref, q_ref, k_ref, v_ref, out_ref, log_ref, masks, total = refs
    else:
        lengths, q_ref, k_ref, v_ref, out_ref, log_ref, masks, total = refs
        images = box_ref = None
    fill_head_masks(masks)
    total[...] = jnp.zeros_like(total)

    def rows_at_once(step, start):
        work = []
        for turn in range(TOGETHER):
            row = TOGETHER * step + turn
            length = lengths[0, row]
            first, offset = row_place(start)
            work.append((row, length, images[0, row] if cross else None, first, offset))
            start = start + length
        picked = [
            dot(pick_rows(offset, length), q_ref[pl.ds(first, WINDOW), :], NN)
            for _, length, _, first, offset in work
        ]
        picked = [(p * HEAD_DIM ** (-0.5)).astype(jnp.bfloat16) for p in picked]
        allowed = [
            cross_allowed(box_ref, row) if cross else self_allowed(offset, length)
            for row, length, _, _, offset in work
        ]
        each = [(turn, group) for turn in range(TOGETHER) for group in range(len(BASES))]
        scores = {}
        for turn, group in each:
            _, _, image, first, _ = work[turn]
            base = BASES[group]
            queries = picked[turn][:, base : base + LANES] * masks[group % 2]
            keys_in = row_keys(cross, first, image, k_ref, base)
            scores[turn, group] = dot(keys_in, queries, NT)
        soft = {}
        for turn, group in each:
            row = work[turn][0]
            masked = jnp.where(allowed[turn], scores[turn, group], -1e30)
            top = jnp.max(masked, axis=0, keepdims=True)
            exps = jnp.exp(masked - top)
            summed = jnp.sum(exps, axis=0, keepdims=True)
            soft[turn, group] = (exps * (1.0 / summed)).astype(jnp.bfloat16)
            log_ref[row, group : group + 1, :] = top + jnp.log(summed)
        mixed = {}
        for turn, group in each:
            _, _, image, first, _ = work[turn]
            values_in = row_keys(cross, first, image, v_ref, BASES[group])
            mixed[turn, group] = (
                dot(soft[turn, group], values_in, TN).astype(jnp.bfloat16) * masks[group % 2]
            )
        for turn in range(TOGETHER):
            _, length, _, first, offset = work[turn]
            side = side_by_side([mixed[turn, group] for group in range(len(BASES))])
            total[pl.ds(first, WINDOW), :] += dot(put_rows(offset, length), side, NN)
        return start

    rows = lengths.shape[1]
    lax.fori_loop(0, rows // TOGETHER, rows_at_once, jnp.int32(0))
    out_ref[...] = total[...].astype(out_ref.dtype)


def backward_kernel(cross, *refs):
    if cross:
        lengths, images, box_ref, key_ref, value_ref = refs[:5]
        refs = refs[5:]
        far_ref, refs = refs[8], refs[:8] + refs[9:]
    else:
        lengths, refs = refs[0], refs[1:]
        images = box_ref = None
    q_ref, k_ref, v_ref, g_ref, log_ref, dq_ref, dk_ref, dv_ref, masks, dq, dk, dv = refs
    fill_head_masks(masks)
    dq[...] = jnp.zeros_like(dq)
    dk[...] = jnp.zeros_like(dk)
    dv[...] = jnp.zeros_like(dv)

    def rows_at_once(step, start):
        work = []
        for turn in range(TOGETHER):
            row = TOGETHER * step + turn
            length = lengths[0, row]
            first, offset = row_place(start)
            work.append((row, length, images[0, row] if cross else None, first, offset))
            start = start + length
        picks = [pick_rows(offset, length) for _, length, _, _, offset in work]
        picked = [
            (dot(pick, q_ref[pl.ds(w[3], WINDOW), :], NN) * HEAD_DIM ** (-0.5)).astype(jnp.bfloat16)
            for pick, w in zip(picks, work)
        ]
        picked_g = [
            dot(pick, g_ref[pl.ds(w[3], WINDOW), :], NN).astype(jnp.bfloat16)
            for pick, w in zip(picks, work)
        ]
        allowed = [
            cross_allowed(box_ref, row) if cross else self_allowed(offset, length)
            for row, length, _, _, offset in work
        ]
        each = [(turn, group) for turn in range(TOGETHER) for group in range(len(BASES))]
        queries, grads, scores, grad_soft = {}, {}, {}, {}
        for turn, group in each:
            _, _, image, first, _ = work[turn]
            base = BASES[group]
            mask = masks[group % 2]
            queries[turn, group] = picked[turn][:, base : base + LANES] * mask
            grads[turn, group] = picked_g[turn][:, base : base + LANES] * mask
            keys_in = row_keys(cross, first, image, k_ref, base)
            values_in = row_keys(cross, first, image, v_ref, base)
            scores[turn, group] = dot(keys_in, queries[turn, group], NT)
            grad_soft[turn, group] = dot(values_in, grads[turn, group], NT)
        soft, grad_scores = {}, {}
        for turn, group in each:
            row = work[turn][0]
            masked = jnp.where(allowed[turn], scores[turn, group], -1e30)
            kept = jnp.exp(masked - log_ref[row, group : group + 1, :])
            inner = jnp.sum(kept * grad_soft[turn, group], axis=0, keepdims=True)
            grad_scores[turn, group] = (kept * (grad_soft[turn, group] - inner)).astype(
                jnp.bfloat16
            )
            soft[turn, group] = kept.astype(jnp.bfloat16)
        grad_k, grad_v, grad_q = {}, {}, {}
        for turn, group in each:
            _, _, image, first, _ = work[turn]
            keys_in = row_keys(cross, first, image, k_ref, BASES[group])
            grad_k[turn, group] = dot(grad_scores[turn, group], queries[turn, group], NN)
            grad_v[turn, group] = dot(soft[turn, group], grads[turn, group], NN)
            grad_q[turn, group] = (
                dot(grad_scores[turn, group], keys_in, TN) * HEAD_DIM ** (-0.5)
            ).astype(jnp.bfloat16) * masks[group % 2]
        for turn in range(TOGETHER):
            _, length, image, first, offset = work[turn]
            every = range(len(BASES))
            side_k = side_by_side([grad_k[turn, group] for group in every])
            side_v = side_by_side([grad_v[turn, group] for group in every])
            side_q = side_by_side([grad_q[turn, group] for group in every])
            if cross:
                dk[image] += side_k
                dv[image] += side_v
            else:
                dk[pl.ds(first, WINDOW), :] += side_k
                dv[pl.ds(first, WINDOW), :] += side_v
            dq[pl.ds(first, WINDOW), :] += dot(put_rows(offset, length), side_q, NN)
        return start

    rows = lengths.shape[1]
    lax.fori_loop(0, rows // TOGETHER, rows_at_once, jnp.int32(0))
    dq_ref[...] = dq[...].astype(dq_ref.dtype)
    dk_ref[...] = dk[...].astype(dk_ref.dtype)
    dv_ref[...] = dv[...].astype(dv_ref.dtype)
    if cross:

        def project(image, _):
            projected = dot(dk_ref[image], key_ref[...], NT) + dot(dv_ref[image], value_ref[...], NT)
            far_ref[image] = projected.astype(far_ref.dtype)
            return _

        lax.fori_loop(0, k_ref.shape[0], project, 0)


def in_smem():
    return pl.BlockSpec(memory_space=pltpu.SMEM)


def in_vmem():
    return pl.BlockSpec(memory_space=pltpu.VMEM)


def attend(scalars, queries, keys_in, values_in, box):
    cross = box is not None
    rows = scalars[0].shape[1]
    tensors = ((box,) if cross else ()) + (queries, keys_in, values_in)
    return pl.pallas_call(
        functools.partial(forward_kernel, cross),
        out_shape=(
            jax.ShapeDtypeStruct(queries.shape, jnp.bfloat16),
            jax.ShapeDtypeStruct((rows, len(BASES), SLOTS), jnp.float32),
        ),
        in_specs=[in_smem()] * len(scalars) + [in_vmem()] * len(tensors),
        out_specs=(in_vmem(), in_vmem()),
        scratch_shapes=[
            pltpu.VMEM((2, SLOTS, LANES), jnp.bfloat16),
            pltpu.VMEM(queries.shape, jnp.float32),
        ],
        compiler_params=pltpu.CompilerParams(vmem_limit_bytes=24 << 20),
        cost_estimate=cost("cross_attend" if cross else "self_attend"),
        name="cross_attend" if cross else "self_attend",
    )(*scalars, *tensors)


def attend_back(scalars, queries, keys_in, values_in, grads, logs, extra=()):
    cross = bool(extra)
    tensors = extra + (queries, keys_in, values_in, grads, logs)
    results = (queries, keys_in, values_in) + ((keys_in,) if cross else ())
    return pl.pallas_call(
        functools.partial(backward_kernel, cross),
        out_shape=tuple(jax.ShapeDtypeStruct(a.shape, jnp.bfloat16) for a in results),
        in_specs=[in_smem()] * len(scalars) + [in_vmem()] * len(tensors),
        out_specs=(in_vmem(),) * len(results),
        scratch_shapes=[
            pltpu.VMEM((2, SLOTS, LANES), jnp.bfloat16),
            pltpu.VMEM(queries.shape, jnp.float32),
            pltpu.VMEM(keys_in.shape, jnp.float32),
            pltpu.VMEM(keys_in.shape, jnp.float32),
        ],
        compiler_params=pltpu.CompilerParams(vmem_limit_bytes=28 << 20),
        cost_estimate=cost("cross_attend_back" if cross else "self_attend_back"),
        name="cross_attend_back" if cross else "self_attend_back",
    )(*scalars, *tensors)


def phi_parts(values):
    size = jnp.abs(values)
    tail = jnp.exp(-0.5 * values * values)
    turn = 1.0 / (1.0 + (0.3275911 * 0.5**0.5) * size)
    series = 1.061405429 * turn - 1.453152027
    series = series * turn + 1.421413741
    series = series * turn - 0.284496736
    series = series * turn + 0.254829592
    half = (0.5 * turn) * series * tail
    return jnp.where(values >= 0, 1.0 - half, half), tail * 0.3989422804014327


def centre(values):
    off = values - jnp.mean(values, axis=-1, keepdims=True)
    scale = lax.rsqrt(jnp.mean(off * off, axis=-1, keepdims=True) + 1e-05)
    return off * scale, scale


def centre_back(grads, normed, scale, gain):
    inner = grads * gain
    mean = jnp.mean(inner, axis=-1, keepdims=True)
    along = jnp.mean(inner * normed, axis=-1, keepdims=True)
    return scale * (inner - mean - normed * along)


def total_rows(values):
    return jnp.sum(values, axis=0, keepdims=True)


def feed_forward_kernel(
    x_ref, xb_ref, expand_ref, reduce_ref, cot_ref, gain_ref, shift_ref,
    active_ref, slope_ref, merged_ref, third_ref, third_b_ref, dgain_ref, dshift_ref, held, acc,
):
    tokens, width = x_ref.shape
    inner = expand_ref.shape[1]
    tiles = inner // FF_TILE

    def hide(tile, slot):
        lanes = pl.ds(pl.multiple_of(tile * FF_TILE, FF_TILE), FF_TILE)
        held[slot] = dot(xb_ref[...], expand_ref[:, lanes], NN)

    def activate(tile, slot):
        lanes = pl.ds(pl.multiple_of(tile * FF_TILE, FF_TILE), FF_TILE)
        hidden = held[slot]
        share, density = phi_parts(hidden)
        active_ref[:, lanes] = (hidden * share).astype(jnp.bfloat16)
        slope_ref[:, lanes] = (share + hidden * density).astype(jnp.bfloat16)

    hide(0, 0)

    def both(pair, _):
        for slot in range(2):
            tile = 2 * pair + slot
            hide(tile + 1, 1 - slot)
            activate(tile, slot)
        return _

    lax.fori_loop(0, tiles // 2 - 1, both, 0)
    hide(tiles - 1, 1)
    activate(tiles - 2, 0)
    activate(tiles - 1, 1)

    def project(tile, _):
        lanes = pl.ds(pl.multiple_of(tile * OUT_TILE, OUT_TILE), OUT_TILE)
        acc[:, lanes] = x_ref[:, lanes] + dot(active_ref[...], reduce_ref[:, lanes], NN)
        return _

    lax.fori_loop(0, width // OUT_TILE, project, 0)
    dgain_ref[...] = jnp.zeros_like(dgain_ref)
    dshift_ref[...] = jnp.zeros_like(dshift_ref)

    def finish(part, _):
        rows = pl.ds(pl.multiple_of(part * ROW_TILE, ROW_TILE), ROW_TILE)
        normed, scale = centre(acc[rows, :])
        merged_ref[rows, :] = (normed * gain_ref[...] + shift_ref[...]).astype(jnp.bfloat16)
        grads = cot_ref[rows, :].astype(jnp.float32)
        third = centre_back(grads, normed, scale, gain_ref[...])
        third_ref[rows, :] = third
        third_b_ref[rows, :] = third.astype(jnp.bfloat16)
        dgain_ref[...] += total_rows(grads * normed)
        dshift_ref[...] += total_rows(grads)
        return _

    lax.fori_loop(0, tokens // ROW_TILE, finish, 0)


def feed_forward(x, xb, expand, reduce, cot, gain, shift):
    tokens, width = x.shape
    inner = expand.shape[1]
    wide = lambda dtype: jax.ShapeDtypeStruct((tokens, inner), dtype)
    square = lambda dtype: jax.ShapeDtypeStruct((tokens, width), dtype)
    flat = jax.ShapeDtypeStruct((1, width), jnp.float32)
    return pl.pallas_call(
        feed_forward_kernel,
        in_specs=[in_vmem()] * 7,
        out_specs=(in_vmem(),) * 7,
        out_shape=(
            wide(jnp.bfloat16), wide(jnp.bfloat16), square(jnp.bfloat16),
            square(jnp.float32), square(jnp.bfloat16), flat, flat,
        ),
        scratch_shapes=[
            pltpu.VMEM((2, tokens, FF_TILE), jnp.float32), pltpu.VMEM((tokens, width), jnp.float32)
        ],
        compiler_params=pltpu.CompilerParams(vmem_limit_bytes=24 << 20),
        cost_estimate=cost("feed_forward"),
        name="feed_forward",
    )(x, xb, expand, reduce, cot, gain[None], shift[None])


def feed_back_kernel(
    third_ref, third_b_ref, slope_ref, expand_ref, reduce_ref, second_ref, gain_ref, cross_out_ref,
    hidden_ref, grad_ref, grad_b_ref, crossed_ref, dgain_ref, dshift_ref, acc,
):
    step = pl.program_id(0)
    active = dot(third_b_ref[...], reduce_ref[...], NT)
    hidden = (active * slope_ref[...].astype(jnp.float32)).astype(jnp.bfloat16)
    hidden_ref[...] = hidden
    part = dot(hidden, expand_ref[...], NT)

    @pl.when(step == 0)
    def _():
        acc[...] = third_ref[...] + part

    @pl.when(step > 0)
    def _():
        acc[...] += part

    @pl.when(step == pl.num_programs(0) - 1)
    def _():
        norm_back(acc, second_ref, gain_ref, grad_ref, grad_b_ref, dgain_ref, dshift_ref)
        crossed_ref[...] = dot(grad_b_ref[...], cross_out_ref[...], NT).astype(jnp.bfloat16)


def norm_back(upstream, summed_ref, gain_ref, grad_ref, grad_b_ref, dgain_ref, dshift_ref):
    dgain_ref[...] = jnp.zeros_like(dgain_ref)
    dshift_ref[...] = jnp.zeros_like(dshift_ref)

    def some_rows(part, _):
        rows = pl.ds(pl.multiple_of(part * ROW_TILE, ROW_TILE), ROW_TILE)
        normed, scale = centre(summed_ref[rows, :])
        grads = upstream[rows, :]
        grad = centre_back(grads, normed, scale, gain_ref[...])
        grad_ref[rows, :] = grad
        grad_b_ref[rows, :] = grad.astype(jnp.bfloat16)
        dgain_ref[...] += total_rows(grads * normed)
        dshift_ref[...] += total_rows(grads)
        return _

    lax.fori_loop(0, summed_ref.shape[0] // ROW_TILE, some_rows, 0)


def feed_back(third, third_b, slope, expand, reduce, second_sum, gain, cross_out):
    tokens, width = third.shape
    inner = expand.shape[1]
    square = lambda dtype: jax.ShapeDtypeStruct((tokens, width), dtype)
    flat = jax.ShapeDtypeStruct((1, width), jnp.float32)
    tile = pl.BlockSpec((tokens, FF_TILE), lambda i: (0, i))
    return pl.pallas_call(
        feed_back_kernel,
        grid=(inner // FF_TILE,),
        in_specs=[
            in_vmem(),
            in_vmem(),
            tile,
            pl.BlockSpec((width, FF_TILE), lambda i: (0, i)),
            pl.BlockSpec((FF_TILE, width), lambda i: (i, 0)),
            in_vmem(),
            in_vmem(),
            in_vmem(),
        ],
        out_specs=(tile,) + (in_vmem(),) * 5,
        out_shape=(
            jax.ShapeDtypeStruct((tokens, inner), jnp.bfloat16), square(jnp.float32),
            square(jnp.bfloat16), square(jnp.bfloat16), flat, flat,
        ),
        scratch_shapes=[pltpu.VMEM((tokens, width), jnp.float32)],
        compiler_params=pltpu.CompilerParams(vmem_limit_bytes=36 << 20),
        cost_estimate=cost("feed_back"),
        name="feed_back",
    )(third, third_b, slope, expand, reduce, second_sum, gain[None], cross_out)


def first_back_kernel(
    gq_ref, query_ref, second_ref, first_ref, gain_ref, output_ref,
    grad_ref, grad_b_ref, attended_ref, dgain_ref, dshift_ref, acc,
):
    acc[...] = second_ref[...] + dot(gq_ref[...], query_ref[...], NT)
    norm_back(acc, first_ref, gain_ref, grad_ref, grad_b_ref, dgain_ref, dshift_ref)
    attended_ref[...] = dot(grad_b_ref[...], output_ref[...], NT).astype(jnp.bfloat16)


def first_back(grad_query, cross_query, grad_second, first_sum, gain, self_output):
    square = lambda dtype: jax.ShapeDtypeStruct(first_sum.shape, dtype)
    flat = jax.ShapeDtypeStruct((1, first_sum.shape[1]), jnp.float32)
    return plain_call(
        first_back_kernel,
        (square(jnp.float32), square(jnp.bfloat16), square(jnp.bfloat16), flat, flat),
        (grad_query, cross_query, grad_second, first_sum, gain[None], self_output),
        [pltpu.VMEM(first_sum.shape, jnp.float32)],
        "first_back",
    )


def plain_call(kernel, out_shape, arrays, scratch, name, scalars=()):
    return pl.pallas_call(
        kernel,
        out_shape=out_shape,
        in_specs=[in_smem()] * len(scalars) + [in_vmem()] * len(arrays),
        out_specs=jax.tree.map(lambda _: in_vmem(), out_shape),
        scratch_shapes=scratch,
        compiler_params=pltpu.CompilerParams(vmem_limit_bytes=24 << 20),
        cost_estimate=cost(name),
        name=name,
    )(*scalars, *arrays)


def text_back_kernel(first_ref, *refs):
    out_ref = refs[-1]
    out_ref[...] = first_ref[...]
    for grad_ref, weight_ref in zip(refs[:3], refs[3:6]):
        out_ref[...] += dot(grad_ref[...], weight_ref[...], NT)


def text_back(grad_first, grads, weights):
    shape = jax.ShapeDtypeStruct(grad_first.shape, jnp.float32)
    return plain_call(text_back_kernel, shape, (grad_first, *grads, *weights), [], "text_back")


def patch_back_kernel(grad_ref, weight_ref, out_ref):
    for image in range(out_ref.shape[0]):
        rows = grad_ref[image * PATCH_ROWS : (image + 1) * PATCH_ROWS]
        out_ref[image] = dot(rows, weight_ref[...], NT)[: out_ref.shape[1]]


def patch_back(grad_projected, vision_proj, shape):
    return plain_call(
        patch_back_kernel,
        jax.ShapeDtypeStruct(shape, jnp.float32),
        (grad_projected, vision_proj),
        [],
        "patch_back",
    )


def terms_of(pieces, arrays, shape, name, turned=None):
    def kernel(core_ref, *refs):
        keep, away = refs[len(arrays) : len(arrays) + 2]
        scratch = refs[len(arrays) + 2 :]

        def put(half, shards, rows, columns, product):
            values = product.astype(jnp.bfloat16)
            values = values.reshape((-1, values.shape[0] // 16 if shards is None else shards[1], values.shape[1]))
            first = slice(None) if shards is None else shards[0]

            def store(ref):
                ref[first, rows, columns] = values

            pl.when(core_ref[0] == half)(lambda: store(keep))
            pl.when(core_ref[0] != half)(lambda: store(away))

        pieces(refs[: len(arrays)], scratch, put)

    out = jax.ShapeDtypeStruct(shape, jnp.bfloat16)
    scratch = [] if turned is None else [pltpu.VMEM(turned, jnp.bfloat16)]
    return plain_call(kernel, (out, out), arrays, scratch, name, (my_bit(*CORE)[None],))


def reduce_terms(refs, scratch, put):
    active, grads = refs
    blocks = active.shape[1] // FF_TILE
    rows = active.shape[1] // 16
    held = 16 // blocks

    def block(at, _):
        lanes = pl.ds(pl.multiple_of(at * FF_TILE, FF_TILE), FF_TILE)
        product = dot(active[:, lanes], grads[...], TN)
        half = product.shape[1] // 2
        shards = (pl.ds(at * held, held), rows)
        put(0, shards, slice(None), slice(None), product[:, :half])
        put(1, shards, slice(None), slice(None), product[:, half:])
        return _

    lax.fori_loop(0, blocks, block, 0)


def expand_terms(refs, scratch, put):
    values, grads = refs
    (turned,) = scratch
    turned[...] = values[...].T
    blocks = grads.shape[1] // FF_TILE

    for at in range(blocks):
        product = dot(turned[...], grads[:, at * FF_TILE : (at + 1) * FF_TILE], NN)
        place = at % (blocks // 2)
        columns = slice(place * FF_TILE, (place + 1) * FF_TILE)
        put(at // (blocks // 2), None, slice(None), columns, product)


def cross_terms(refs, scratch, put):
    crossed, grad_second, normed_one, grad_query, far, grad_key, grad_value = refs
    width = crossed.shape[1]
    left, right = slice(0, width), slice(width, 2 * width)
    put(0, None, slice(None), left, dot(crossed[...], grad_second[...], TN))
    put(0, None, slice(None), right, dot(normed_one[...], grad_query[...], TN))
    put(1, None, slice(None), left, dot(far[...], grad_key[...], TN))
    put(1, None, slice(None), right, dot(far[...], grad_value[...], TN))


def pair_terms(refs, scratch, put):
    left, left_grad, right, right_grad = refs
    every = slice(None)
    put(0, None, every, every, dot(left[...], left_grad[...], TN))
    put(1, None, every, every, dot(right[...], right_grad[...], TN))


def vision_terms(refs, scratch, put):
    patches, grads = refs
    half = patches.shape[1] // 2
    every = slice(None)
    put(0, None, every, every, dot(patches[:, :half], grads[...], TN))
    put(1, None, every, every, dot(patches[:, half:], grads[...], TN))


def box_columns(box_mask, patch_rows):
    turned = jnp.transpose(box_mask).astype(jnp.bfloat16)
    return jnp.pad(
        turned, ((0, patch_rows - turned.shape[0]), (0, SLOTS - turned.shape[1]))
    )


def flip_bit(values, axis, bit):
    count = lax.axis_size(axis)
    return lax.ppermute(values, axis, [(i, i ^ (1 << bit)) for i in range(count)])


def my_bit(axis, bit):
    return (lax.axis_index(axis) >> bit) & 1


def stage_order(names):
    bits = {"x": [("dp", 1)], "y": [("mod", 0)], "z": [("dp", 2), ("dp", 3)]}
    return sum([bits[name] for name in names], [])


def other_bits():
    dp_bits = lax.axis_size("dp").bit_length() - 1
    mod_bits = lax.axis_size("mod").bit_length() - 1
    return [("mod", bit) for bit in range(1, mod_bits)] + [("dp", bit) for bit in range(4, dp_bits)]


CORE = ("dp", 0)
ORDERS = {"r": "yxz", "e": "zxy", "c": "xyz", "s": "yxz", "q": "xyz", "v": "xyz"}
TURNS = "PergAvcrTvscvgerqvcesvrcgvesqvcesvrcseqgvsVqsqcsrqeqsRSqceCEqQ"


def place_in(order):
    place = jnp.int32(0)
    for axis, bit in order:
        place = 2 * place + my_bit(axis, bit)
    return place


class Sum:
    def __init__(self, keep, away, order):
        self.order = order = stage_order(order)
        self.kept = keep
        self.flown = flip_bit(away, *CORE)
        self.steps = [("scatter", stage) for stage in order]
        self.steps += [("add", stage) for stage in other_bits()]
        self.steps += [("gather", stage) for stage in reversed(order)] + [("last", CORE)]
        self.before = "add"

    def advance(self):
        if self.before == "add":
            values = self.kept + self.flown
        else:
            values = jnp.concatenate([self.kept, self.flown], axis=0)
        kind, (axis, bit) = self.steps.pop(0)
        if kind == "scatter":
            mine = my_bit(axis, bit)
            pair = values.reshape((2, values.shape[0] // 2) + values.shape[1:])
            away = lax.dynamic_index_in_dim(pair, 1 - mine, 0, False)
            self.kept = lax.dynamic_index_in_dim(pair, mine, 0, False)
        else:
            self.kept = away = values
        self.flown = flip_bit(away, axis, bit)
        self.before = "add" if kind in ("scatter", "add") else "gather"


class Line:
    def __init__(self):
        self.token = jnp.zeros((1, 1), jnp.float32)

    def meet(self, values, *sums):
        flown = [one.flown for one in sums]
        values, self.token, flown = lax.optimization_barrier((values, self.token, flown))
        for one, arrived in zip(sums, flown):
            one.flown = arrived
            if one.steps:
                one.advance()
        return values


class SmallSum:
    def __init__(self, values):
        self.steps = [CORE] + stage_order("xyz") + other_bits()
        self.kept = values
        self.flown = jnp.zeros_like(values)
        self.advance()

    def advance(self):
        self.kept = self.kept + self.flown
        self.flown = flip_bit(self.kept, *self.steps.pop(0))

    @property
    def total(self):
        return self.kept + self.flown


def spread(one, shapes, fill, name):
    own, other = one.kept, one.flown
    shards, rows, columns = own.shape
    at = jnp.stack([my_bit(*CORE), place_in(one.order)])

    def kernel(at_ref, own_ref, other_ref, *outs):
        inner = at_ref[1] & 3

        def write(low, high):
            for step in range(4):
                fill(low.at[step ^ inner], high.at[step ^ inner], outs, step)

        pl.when(at_ref[0] == 0)(lambda: write(own_ref, other_ref))
        pl.when(at_ref[0] == 1)(lambda: write(other_ref, own_ref))

    def block_of(shape):
        lead = len(shape) - 3
        return pl.BlockSpec(
            shape[:lead] + (4,) + shape[lead + 1 :],
            lambda i, at_ref: (0,) * lead + (i, 0, 0),
        )

    taken = pl.BlockSpec((4, rows, columns), lambda i, at_ref: (i ^ (at_ref[1] >> 2), 0, 0))
    return pl.pallas_call(
        kernel,
        out_shape=tuple(jax.ShapeDtypeStruct(shape, jnp.float32) for shape in shapes),
        grid_spec=pltpu.PrefetchScalarGridSpec(
            num_scalar_prefetch=1,
            grid=(shards // 4,),
            in_specs=[taken, taken],
            out_specs=tuple(block_of(shape) for shape in shapes),
        ),
        compiler_params=pltpu.CompilerParams(vmem_limit_bytes=24 << 20),
        cost_estimate=pl.CostEstimate(
            flops=0, bytes_accessed=12 * own.size, transcendentals=0
        ),
        name=name,
    )(at, own, other)


def fill_columns(low, high, outs, step):
    columns = low.shape[-1]
    outs[0][step, :, :columns] = low[...].astype(jnp.float32)
    outs[0][step, :, columns:] = high[...].astype(jnp.float32)


def fill_couples(low, high, outs, step):
    columns = low.shape[-1] // 2
    for half, taken in enumerate((low, high)):
        outs[2 * half][step] = taken[:, :columns].astype(jnp.float32)
        outs[2 * half + 1][step] = taken[:, columns:].astype(jnp.float32)


def fill_each(low, high, outs, step):
    outs[0][step] = low[...].astype(jnp.float32)
    outs[1][step] = high[...].astype(jnp.float32)


def fill_halves(low, high, outs, step):
    outs[0][0, step] = low[...].astype(jnp.float32)
    outs[0][1, step] = high[...].astype(jnp.float32)


def on_device(
    text_tokens,
    patches,
    lengths,
    row_image,
    box_mask,
    cotangent,
    self_query,
    self_key,
    self_value,
    self_output,
    first_gain,
    first_bias,
    cross_query,
    cross_key,
    cross_value,
    cross_output,
    second_gain,
    second_bias,
    expand_weight,
    reduce_weight,
    third_gain,
    third_bias,
    vision_proj,
):
    image_count = patches.shape[0]
    box = box_columns(box_mask[0], PATCH_ROWS)
    patch_count = patches.shape[1]
    flat_patches = jnp.pad(patches, ((0, 0), (0, PATCH_ROWS - patch_count), (0, 0))).reshape(
        image_count * PATCH_ROWS, patches.shape[2]
    )

    def by_image(values):
        return values.reshape(image_count, PATCH_ROWS, values.shape[-1])

    projected = matmul(flat_patches, vision_proj).astype(jnp.bfloat16)
    far_projected = flip_bit(projected, "mod", 0)
    query_s = matmul(text_tokens, self_query).astype(jnp.bfloat16)
    key_s = matmul(text_tokens, self_key).astype(jnp.bfloat16)
    value_s = matmul(text_tokens, self_value).astype(jnp.bfloat16)
    attended_b, self_log = attend((lengths,), query_s, key_s, value_s, None)
    first_sum = text_tokens.astype(jnp.float32) + matmul(attended_b, self_output)
    normed_one = norm_rows(first_sum, first_gain, first_bias)
    normed_one_b = normed_one.astype(jnp.bfloat16)
    query_c = matmul(normed_one_b, cross_query).astype(jnp.bfloat16)
    far_keys = by_image(matmul(far_projected, cross_key).astype(jnp.bfloat16))
    far_values = by_image(matmul(far_projected, cross_value).astype(jnp.bfloat16))
    crossed_b, cross_log = attend((lengths, row_image), query_c, far_keys, far_values, box)
    second_sum = normed_one + matmul(crossed_b, cross_output)
    normed_two = norm_rows(second_sum, second_gain, second_bias)
    normed_two_b = normed_two.astype(jnp.bfloat16)
    activated_b, slope, merged, grad_third, grad_third_b, grad_third_gain, grad_third_bias = (
        feed_forward(
            normed_two, normed_two_b, expand_weight, reduce_weight, cotangent, third_gain, third_bias
        )
    )
    line = Line()
    width = text_tokens.shape[1]
    inner = expand_weight.shape[1]
    sums = {}
    sums["r"] = Sum(
        *terms_of(
            reduce_terms, (activated_b, grad_third_b), (16, inner // 16, width // 2), "reduce_terms"
        ),
        ORDERS["r"],
    )
    (
        grad_hidden,
        grad_second,
        grad_second_b,
        grad_crossed,
        grad_second_gain,
        grad_second_bias,
    ) = feed_back(
        grad_third,
        grad_third_b,
        slope,
        expand_weight,
        reduce_weight,
        second_sum,
        second_gain,
        cross_output,
    )
    grad_hidden, grad_crossed = line.meet((grad_hidden, grad_crossed), sums["r"])
    sums["e"] = Sum(
        *terms_of(
            expand_terms,
            (normed_two_b, grad_hidden),
            (16, width // 16, inner // 2),
            "expand_terms",
            normed_two_b.shape,
        ),
        ORDERS["e"],
    )
    grad_crossed, sums["e"].kept = line.meet((grad_crossed, sums["e"].kept))
    grads_cross = attend_back(
        (lengths, row_image),
        query_c,
        far_keys,
        far_values,
        grad_crossed,
        cross_log,
        (box, cross_key, cross_value),
    )
    grads_cross = line.meet(grads_cross, sums["e"], sums["r"])
    grad_query_c, grad_far_keys, grad_far_values, grad_far_projected = grads_cross
    grad_far_keys = grad_far_keys.reshape(projected.shape)
    grad_far_values = grad_far_values.reshape(projected.shape)
    grad_projected = flip_bit(grad_far_projected.reshape(projected.shape), "mod", 0)
    grad_first, grad_first_b, grad_attended, grad_first_gain, grad_first_bias = first_back(
        grad_query_c, cross_query, grad_second, first_sum, first_gain, self_output
    )
    small_sum = SmallSum(
        jnp.concatenate(
            [
                grad_first_gain,
                grad_first_bias,
                grad_second_gain,
                grad_second_bias,
                grad_third_gain,
                grad_third_bias,
            ]
        )
    )
    sums["g"] = small_sum
    grad_attended, grad_far_values = line.meet((grad_attended, grad_far_values))
    sums["c"] = Sum(
        *terms_of(
            cross_terms,
            (
                crossed_b,
                grad_second_b,
                normed_one_b,
                grad_query_c,
                far_projected,
                grad_far_keys,
                grad_far_values,
            ),
            (16, width // 16, 2 * width),
            "cross_terms",
        ),
        ORDERS["c"],
    )
    grad_attended = line.meet(grad_attended, sums["r"])
    grad_attended = line.meet(grad_attended, sums["c"], sums["g"])
    patch_grad = patch_back(grad_projected, vision_proj, patches.shape)
    half = vision_proj.shape[0] // 2
    tall = (16, half // 16, width)
    sums["v"] = Sum(
        *terms_of(vision_terms, (flat_patches, grad_projected), tall, "vision_terms"), ORDERS["v"]
    )
    square = (16, width // 16, width)

    def pair_sum(name, order, *arrays):
        return Sum(*terms_of(pair_terms, arrays, square, name), order)

    spreads = {}
    for turn in TURNS:
        if turn == "A":
            grad_attended = line.meet(grad_attended)
            grads_self = attend_back((lengths,), query_s, key_s, value_s, grad_attended, self_log)
            grads_self = line.meet(grads_self)
            grad_query_s, grad_key_s, grad_value_s = grads_self
            sums["s"] = pair_sum(
                "self_terms_one", ORDERS["s"], attended_b, grad_first_b, text_tokens, grad_key_s
            )
            sums["q"] = pair_sum(
                "self_terms_two", ORDERS["q"], text_tokens, grad_query_s, text_tokens, grad_value_s
            )
            text_grad = text_back(grad_first, grads_self, (self_query, self_key, self_value))
        elif turn == "T":
            text_grad = line.meet(text_grad)
        elif turn == "P":
            patch_grad = line.meet(patch_grad)
        elif turn.isupper():
            one = sums[turn.lower()]
            while one.steps:
                line.meet((), one)
            line.meet((), one)
            shapes, fill = {
                "R": ([(16,) + (inner // 16, width)], fill_columns),
                "E": ([(16,) + (width // 16, inner)], fill_columns),
                "C": ([square] * 4, fill_couples),
                "S": ([square] * 2, fill_each),
                "Q": ([square] * 2, fill_each),
                "V": ([(2,) + tall], fill_halves),
            }[turn]
            spreads[turn] = line.meet(spread(one, shapes, fill, "spread_" + turn.lower()))
        else:
            line.meet((), sums[turn])
    while small_sum.steps:
        line.meet((), small_sum)
    small = line.meet(small_sum.total) + line.token
    (sum_reduce,) = spreads["R"]
    (sum_expand,) = spreads["E"]
    sum_cross_output, sum_cross_query, sum_cross_key, sum_cross_value = spreads["C"]
    sum_self_output, sum_self_key = spreads["S"]
    sum_self_query, sum_self_value = spreads["Q"]
    (sum_vision,) = spreads["V"]

    def whole(values, like):
        return values.reshape(like.shape)

    return (
        merged,
        text_grad,
        patch_grad,
        whole(sum_self_query, self_query),
        whole(sum_self_key, self_key),
        whole(sum_self_value, self_value),
        whole(sum_self_output, self_output),
        small[0],
        small[1],
        whole(sum_cross_query, cross_query),
        whole(sum_cross_key, cross_key),
        whole(sum_cross_value, cross_value),
        whole(sum_cross_output, cross_output),
        small[2],
        small[3],
        whole(sum_expand, expand_weight),
        whole(sum_reduce, reduce_weight),
        small[4],
        small[5],
        whole(sum_vision, vision_proj),
    )


def solution(mesh):
    placed = (
        P(("mod", "dp"), None),
        P(("mod", "dp"), None, None),
        P(("mod", "dp"), None),
        P(("mod", "dp"), None),
        P(("mod", "dp"), None, None),
        P(("mod", "dp"), None),
        P(),
        P(),
        P(),
        P(),
        P(),
        P(),
        P(),
        P(),
        P(),
        P(),
        P(),
        P(),
        P(),
        P(),
        P(),
        P(),
        P(),
    )
    return jax.shard_map(
        on_device,
        mesh=mesh,
        in_specs=placed,
        out_specs=(
            P(("mod", "dp"), None),
            P(("mod", "dp"), None),
            P(("mod", "dp"), None, None),
            P(),
            P(),
            P(),
            P(),
            P(),
            P(),
            P(),
            P(),
            P(),
            P(),
            P(),
            P(),
            P(),
            P(),
            P(),
            P(),
            P(),
        ),
        check_vma=False,
    )
```
